128 devices in a mesh: tm: 64 (over y, x, z), head: 2 (over core).
Axes of the slice: x: 4, y: 4, z: 4, core: 2. Of those that a mesh axis runs over, the one named last changes fastest.
Arguments:
- frames: bfloat16 [65536, 1024], P(('tm', 'head')), may hold values from -6 to 6
- conv_in: bfloat16 [1024, 2048], replicated, may hold values from -0.1875 to 0.1875
- depth_taps: float32 [31, 1024], replicated, may hold values from -1 to 1
- conv_out: bfloat16 [1024, 1024], replicated, may hold values from -0.1875 to 0.1875
- w_query: bfloat16 [1024, 1024], P(None, 'head'), may hold values from -0.1875 to 0.1875
- w_key: bfloat16 [1024, 1024], P(None, 'head'), may hold values from -0.1875 to 0.1875
- w_value: bfloat16 [1024, 1024], P(None, 'head'), may hold values from -0.1875 to 0.1875
- feature_map: bfloat16 [8, 128, 256], P('head'), may hold values from -0.5 to 0.5
- w_out: bfloat16 [1024, 1024], P('head'), may hold values from -0.1875 to 0.1875
Outputs:
- encoded: bfloat16 [65536, 1024], P(('tm', 'head'))
The draws below stay inside these ranges and needn't reach their ends.
All inputs are finite; a program needn't handle non-finite values.
Results may differ from the reference program's by a relative error of at most 0.0085.
Values may be sent and summed in bfloat16 or wider, within the bound.
A program may use at most 128 MiB of HBM per device.

```python
import jax
import jax.numpy as jnp
from jax import lax

D = 1024
HEADS = 8
HEAD_DIM = 128
FEAT = 256
TAPS = 31
BLK = 512
FRAMES = 65536


def block_scale(rng, extent, pieces, smallest, high):
    factor_of, own = 1.0, jax.random.fold_in(rng, 6)
    for axis_at, shards_of in pieces:
        steps = jnp.exp(jax.random.uniform(jax.random.fold_in(own, axis_at), (shards_of,), jnp.float32, smallest / len(pieces), high / len(pieces)))
        factor_of = factor_of * jnp.repeat(steps, extent[axis_at] // shards_of).reshape([-1 if axis == axis_at else 1 for axis in range(len(extent))])
    return factor_of


def normal_values(own_key, dims, deviation, most, pieces=(), held_as=jnp.bfloat16):
    array = deviation * jax.random.normal(own_key, dims, jnp.float32)
    if pieces:
        array = array * block_scale(own_key, dims, pieces, -0.22, 0.18)
    return jnp.clip(array, -most, most).astype(held_as)


def setup_inputs(seed: int = 0) -> dict:
    streams_of = jax.random.split(jax.random.key(seed), 10)
    frames = normal_values(streams_of[0], (FRAMES, D), 1.0, 6.0, ((0, 128),))
    conv_in = normal_values(streams_of[1], (D, 2 * D), D ** -0.5, 0.1875)
    depth_taps = normal_values(streams_of[2], (TAPS, D), TAPS ** -0.5, 1.0, (), jnp.float32)
    conv_out = normal_values(streams_of[3], (D, D), D ** -0.5, 0.1875)
    w_query = normal_values(streams_of[4], (D, HEADS * HEAD_DIM), D ** -0.5, 0.1875, ((1, 2),))
    w_key = normal_values(streams_of[5], (D, HEADS * HEAD_DIM), D ** -0.5, 0.1875, ((1, 2),))
    w_value = normal_values(streams_of[6], (D, HEADS * HEAD_DIM), D ** -0.5, 0.1875, ((1, 2),))
    feature_map = normal_values(streams_of[7], (HEADS, HEAD_DIM, FEAT), HEAD_DIM ** -0.5, 0.5, ((0, 2),))
    w_out = normal_values(streams_of[8], (HEADS * HEAD_DIM, D), (HEADS * HEAD_DIM) ** -0.5, 0.1875, ((0, 2),))
    return dict(frames=frames, conv_in=conv_in, depth_taps=depth_taps, conv_out=conv_out, w_query=w_query, w_key=w_key, w_value=w_value, feature_map=feature_map, w_out=w_out)


def layer_norm(values):
    center = values - lax.optimization_barrier(jnp.mean(values, axis=-1, keepdims=True))
    spread = lax.optimization_barrier(jnp.mean(center * center, axis=-1, keepdims=True))
    return center * lax.rsqrt(spread + 1e-05)

def reference(frames, conv_in, depth_taps, conv_out, w_query, w_key, w_value, feature_map, w_out):
    highest = lax.Precision.HIGHEST
    inputs = frames.astype(jnp.float32)
    count = inputs.shape[0]
    normed = layer_norm(inputs).astype(jnp.bfloat16)
    projected = jnp.dot(normed, conv_in, preferred_element_type=jnp.float32)
    glu_out = (projected[:, :D] * jax.nn.sigmoid(projected[:, D:])).astype(jnp.bfloat16)
    reach = TAPS // 2
    padded = jnp.pad(glu_out.astype(jnp.float32), ((reach, reach), (0, 0)))
    depthwise = jnp.zeros((count, D), jnp.float32)
    for offset in range(TAPS):
        depthwise = depthwise + depth_taps[offset] * padded[offset:offset + count]
    activated = jax.nn.silu(layer_norm(depthwise)).astype(jnp.bfloat16)
    middle = (inputs + jnp.dot(activated, conv_out, preferred_element_type=jnp.float32)).astype(jnp.bfloat16)
    attn_in = layer_norm(middle.astype(jnp.float32)).astype(jnp.bfloat16)
    query = jnp.dot(attn_in, w_query, preferred_element_type=jnp.float32).astype(jnp.bfloat16)
    key = jnp.dot(attn_in, w_key, preferred_element_type=jnp.float32).astype(jnp.bfloat16)
    value = jnp.dot(attn_in, w_value, preferred_element_type=jnp.float32).astype(jnp.bfloat16)
    query = query.reshape(count, HEADS, HEAD_DIM)
    key = key.reshape(count, HEADS, HEAD_DIM)
    value = value.reshape(count, HEADS, HEAD_DIM)
    fmap = feature_map.astype(jnp.float32)
    query_map = jax.nn.silu(jnp.einsum('thd,hdf->thf', query.astype(jnp.float32), fmap, precision=highest)).astype(jnp.bfloat16)
    key_map = jax.nn.silu(jnp.einsum('thd,hdf->thf', key.astype(jnp.float32), fmap, precision=highest)).astype(jnp.bfloat16)
    blocks = count // BLK
    query_map = query_map.reshape(blocks, BLK, HEADS, FEAT)
    key_map = key_map.reshape(blocks, BLK, HEADS, FEAT)
    value = value.reshape(blocks, BLK, HEADS, HEAD_DIM)
    causal = jnp.arange(BLK)[:, None] >= jnp.arange(BLK)[None, :]

    def advance(state, inputs_block):
        query_block, key_block, value_block = inputs_block
        query_wide = query_block.astype(jnp.float32)
        key_wide = key_block.astype(jnp.float32)
        value_wide = value_block.astype(jnp.float32)
        inter = jnp.einsum('thf,hfd->thd', query_wide, state, precision=highest)
        scores = jnp.einsum('thf,shf->hts', query_wide, key_wide, precision=highest)
        weights = jnp.where(causal[None], scores, 0.0).astype(jnp.bfloat16).astype(jnp.float32)
        intra = jnp.einsum('hts,shd->thd', weights, value_wide, precision=highest)
        state = state + jnp.einsum('shf,shd->hfd', key_wide, value_wide, precision=highest)
        return (state, inter + intra)
    start_state = jnp.zeros((HEADS, FEAT, HEAD_DIM), jnp.float32)
    final_state, numerator = lax.scan(advance, start_state, (query_map, key_map, value))
    numerator = numerator.reshape(count, HEADS, HEAD_DIM)
    scale = lax.rsqrt(lax.optimization_barrier(jnp.mean(numerator * numerator, axis=-1, keepdims=True)) + 1e-06)
    attended = (numerator * scale).astype(jnp.bfloat16).reshape(count, HEADS * HEAD_DIM)
    branch = jnp.dot(attended, w_out, preferred_element_type=jnp.float32)
    return (middle.astype(jnp.float32) + branch).astype(jnp.bfloat16)
```

```python
import functools

import jax
import jax.numpy as jnp
from jax import lax
from jax.experimental import pallas as pl
from jax.experimental.pallas import tpu as pltpu
from jax.sharding import Mesh
from jax.sharding import PartitionSpec as P

AXES = ("tm_0", "tm_1", "tm_2", "head")
MESH = pl.DeviceIdType.MESH
BF16 = jnp.bfloat16
F32 = jnp.float32

ROWS = 512
D = 1024
HALO = 16
PAD = ROWS + 2 * HALO
HALF = 512
HEADS = 4
HD = 128
FEAT = 256
TAPS = 31
CHUNK = 256


def dot(a, b):
    return jnp.dot(a, b, preferred_element_type=F32)


def dot_nt(a, b):
    return lax.dot_general(a, b, (((1,), (1,)), ((), ())), preferred_element_type=F32)


def sigmoid(v):
    return 0.5 * jnp.tanh(0.5 * v) + 0.5


def silu(v):
    half = 0.5 * v
    return half * jnp.tanh(half) + half


def layer_norm(values):
    center = values - jnp.mean(values, axis=-1, keepdims=True)
    spread = jnp.mean(center * center, axis=-1, keepdims=True)
    return center * lax.rsqrt(spread + 1e-05)


def kernel(
    sizes,
    frames, conv_in, taps, conv_out, wq, wk, wv, fm, wo, out,
    xp, normed, w_in, tap_v, w_c, wq_v, wk_v, wv_v, fm_v, wo_v, fmt,
    glu, dw, act, mid, attn, proj, val, kmapt, num, att, acc, obuf,
    st_own, p_send, p_recv, a_send, a_recv, y_send, y_recv, r_send, r_recv, pref, q_send, q_recv,
    load_sem, halo_s, halo_r, w_s, w_r, pq_s, pq_r, a_s, a_r, y_s, y_r, r_s, r_r,
):
    ny, nx, nz = sizes
    planes = nx * nz
    count = ny * planes * 2
    y, x, z, h = [lax.axis_index(a) for a in AXES]
    plane = x * nz + z
    lin = ((y * nx + x) * nz + z) * 2 + h
    other = 1 - h
    pair = (y, x, z, other)

    def device(n):
        chip = lax.div(n, 2)
        column = lax.rem(chip, planes)
        return (lax.div(chip, planes), lax.div(column, nz), lax.rem(column, nz), lax.rem(n, 2))

    prev = device(lax.rem(lin + count - 1, count))
    following = device(lax.rem(lin + 1, count))

    def plane_peer(k):
        p = lax.rem(plane + k, planes)
        return (y, lax.div(p, nz), lax.rem(p, nz), h)

    def y_peer(k):
        return (lax.rem(y + k, ny), x, z, h)

    loads = []

    def load(src, dst):
        copy = pltpu.make_async_copy(src, dst, load_sem.at[len(loads)])
        copy.start()
        loads.append(copy)
        return copy

    ld_x = load(frames, xp.at[pl.ds(HALO, ROWS)])
    ld_in = []
    for c in range(8):
        at = (c % 2) * 4 + c // 2
        ld_in.append(load(conv_in.at[:, pl.ds(at * CHUNK, CHUNK)], w_in.at[at]))
    ld_tap = load(taps, tap_v)
    ld_c = load(conv_out, w_c)
    ld_k = load(wk, wk_v.at[h])
    ld_v = load(wv, wv_v.at[h])
    ld_f = load(fm, fm_v.at[h])
    ld_q = load(wq, wq_v.at[h])
    ld_o = load(wo, wo_v.at[h])

    barrier = pltpu.get_barrier_semaphore()

    def greet(d):
        pl.semaphore_signal(barrier, inc=1, device_id=d, device_id_type=MESH)

    greet(prev)
    greet(following)
    greet(pair)

    @pl.loop(1, planes)
    def _(k):
        greet(plane_peer(k))

    for k in range(1, ny):
        greet(y_peer(k))
    pl.semaphore_wait(barrier, 3 + planes - 1 + ny - 1)

    def remote(src, dst, s, r, d):
        return pltpu.make_async_remote_copy(
            src_ref=src, dst_ref=dst, send_sem=s, recv_sem=r, device_id=d, device_id_type=MESH
        )

    halo_low = remote(
        frames.at[pl.ds(0, HALO)], xp.at[pl.ds(HALO + ROWS, HALO)], halo_s.at[0], halo_r.at[0], prev
    )
    halo_high = remote(
        frames.at[pl.ds(ROWS - HALO, HALO)], xp.at[pl.ds(0, HALO)], halo_s.at[1], halo_r.at[1], following
    )
    halo_low.start()
    halo_high.start()
    weights = []
    for i, (src, dst) in enumerate(((wk, wk_v), (wv, wv_v), (fm, fm_v), (wq, wq_v), (wo, wo_v))):
        copy = remote(src, dst.at[h], w_s.at[i], w_r.at[i], pair)
        copy.start()
        weights.append(copy)

    ld_x.wait()

    @pl.loop(0, ROWS // 32)
    def _(i):
        at = pl.ds(pl.multiple_of(HALO + i * 32, 16), 32)
        normed[at, :] = layer_norm(xp[at, :].astype(F32)).astype(BF16)

    halo_low.wait()
    halo_high.wait()
    top = layer_norm(xp[pl.ds(0, HALO), :].astype(F32))
    normed[pl.ds(0, HALO), :] = jnp.where(lin == 0, 0.0, top).astype(BF16)
    bottom = layer_norm(xp[pl.ds(HALO + ROWS, HALO), :].astype(F32))
    normed[pl.ds(HALO + ROWS, HALO), :] = jnp.where(lin == count - 1, 0.0, bottom).astype(BF16)

    for c in range(4):
        ld_in[2 * c].wait()
        ld_in[2 * c + 1].wait()
        value = dot(normed[...], w_in[c])
        gate = dot(normed[...], w_in[4 + c])
        glu[:, c * CHUNK : (c + 1) * CHUNK] = (value * sigmoid(gate)).astype(BF16).astype(F32)

    ld_tap.wait()
    rb = 64

    @pl.loop(0, ROWS // rb)
    def _(i):
        base = pl.multiple_of(i * rb, rb)
        for c in range(D // 128):
            cols = slice(c * 128, (c + 1) * 128)
            window = glu[pl.ds(base, rb + 32), cols]
            total = None
            for r in range(8):
                part = None
                for q in range(4):
                    j = 8 * q + r - 1
                    if j < 0:
                        continue
                    term = window[8 * q : 8 * q + rb + 8] * tap_v[j : j + 1, cols]
                    part = term if part is None else part + term
                part = part[r : r + rb]
                total = part if total is None else total + part
            dw[pl.ds(base, rb), cols] = total
        act[pl.ds(base, rb), :] = silu(layer_norm(dw[pl.ds(base, rb), :])).astype(BF16)

    ld_c.wait()
    for c in range(4):
        cols = slice(c * CHUNK, (c + 1) * CHUNK)
        mid[:, cols] = (
            xp[pl.ds(HALO, ROWS), cols].astype(F32) + dot(act[...], w_c[:, cols])
        ).astype(BF16)

    @pl.loop(0, ROWS // 32)
    def _(i):
        at = pl.ds(pl.multiple_of(i * 32, 32), 32)
        attn[at, :] = layer_norm(mid[at, :].astype(F32)).astype(BF16)

    def half_states(half, emit):
        for c in range(2):
            cols = slice(c * CHUNK, (c + 1) * CHUNK)
            proj[:, cols] = dot(attn[...], wk_v[half, :, cols]).astype(BF16)
            val[half, :, cols] = dot(attn[...], wv_v[half, :, cols]).astype(BF16)
        for e in range(HEADS):
            cols = slice(e * HD, (e + 1) * HD)
            fmt[half, e] = fm_v[half, e].astype(F32).T.astype(BF16)
            kt = silu(dot_nt(fmt[half, e], proj[:, cols])).astype(BF16)
            kmapt[half, e] = kt
            emit(e, dot(kt, val[half, :, cols]))

    ld_k.wait()
    ld_v.wait()
    ld_f.wait()
    for copy in weights[:3]:
        copy.wait()

    def emit_other(e, s):
        p_send[e] = s.astype(BF16)

    def emit_own(e, s):
        st_own[e] = s

    half_states(other, emit_other)
    p_copy = remote(p_send, p_recv, pq_s.at[0], pq_r.at[0], pair)
    p_copy.start()
    half_states(h, emit_own)
    p_copy.wait()

    piece = HEADS * FEAT // planes
    per = planes // HEADS
    for e in range(HEADS):
        chip_state = (st_own[e] + p_recv[e].astype(F32)).astype(BF16)
        a_send[e * per : (e + 1) * per] = chip_state.reshape(per, piece, HD)

    def a_copy(k):
        p = lax.rem(plane + k, planes)
        return remote(a_send.at[p], a_recv.at[plane], a_s.at[k], a_r.at[k], plane_peer(k))

    @pl.loop(1, planes)
    def _(k):
        a_copy(k).start()

    a_recv[plane] = a_send[plane]

    ld_q.wait()
    ld_o.wait()
    weights[3].wait()
    weights[4].wait()

    def half_project(half):
        for c in range(2):
            cols = slice(c * CHUNK, (c + 1) * CHUNK)
            proj[:, cols] = dot(attn[...], wq_v[half, :, cols]).astype(BF16)

    side = ROWS // 2
    causal = lax.broadcasted_iota(jnp.int32, (side, side), 0) >= lax.broadcasted_iota(
        jnp.int32, (side, side), 1
    )

    def half_intra(half, qmaps):
        for e in range(HEADS):
            cols = slice(e * HD, (e + 1) * HD)
            qmaps[e] = silu(dot(proj[:, cols], fm_v[half, e])).astype(BF16)
            w00 = jnp.where(causal, dot(qmaps[e, :side], kmapt[half, e, :, :side]), 0.0).astype(BF16)
            num[half, e, :side] = dot(w00, val[half, :side, cols])
            w10 = dot(qmaps[e, side:], kmapt[half, e, :, :side]).astype(BF16)
            w11 = jnp.where(causal, dot(qmaps[e, side:], kmapt[half, e, :, side:]), 0.0).astype(BF16)
            num[half, e, side:] = dot(w10, val[half, :side, cols]) + dot(w11, val[half, side:, cols])

    q_other = att.at[0]
    q_own = att.at[1]
    half_project(other)
    half_intra(other, q_other)

    @pl.loop(1, planes)
    def _(k):
        a_copy(k).wait()

    run = a_recv[0].astype(F32)
    for p in range(1, planes):
        run = run + a_recv[p].astype(F32)
    y_send[...] = run

    def y_copy(k):
        return remote(y_send, y_recv.at[y], y_s.at[k], y_r.at[k], y_peer(k))

    for k in range(1, ny):
        y_copy(k).start()

    half_project(h)

    for k in range(1, ny):
        y_copy(k).wait()
    run = jnp.zeros((piece, HD), F32)
    for k in range(1, ny):
        src = lax.rem(y + ny - k, ny)
        run = run + jnp.where(src < y, y_recv[src], 0.0)
    for p in range(planes):
        r_send[p] = run.astype(BF16)
        run = run + a_recv[p].astype(F32)

    def r_copy(k):
        p = lax.rem(plane + k, planes)
        return remote(r_send.at[p], r_recv.at[plane], r_s.at[k], r_r.at[k], plane_peer(k))

    @pl.loop(1, planes)
    def _(k):
        r_copy(k).start()

    r_recv[plane] = r_send[plane]

    half_intra(h, q_own)

    @pl.loop(1, planes)
    def _(k):
        r_copy(k).wait()

    for e in range(HEADS):
        before = r_recv[e * per : (e + 1) * per].reshape(FEAT, HD).astype(F32)
        q_send[e] = (before + jnp.where(h == 0, st_own[e], 0.0)).astype(BF16)
        pref[e] = (before + jnp.where(h == 1, p_recv[e].astype(F32), 0.0)).astype(BF16)
    q_copy = remote(q_send, q_recv, pq_s.at[1], pq_r.at[1], pair)
    q_copy.start()

    def half_inter(half, qmaps, prefix):
        for e in range(HEADS):
            numerator = num[half, e] + dot(qmaps[e], prefix[e])
            scale = lax.rsqrt(jnp.mean(numerator * numerator, axis=-1, keepdims=True) + 1e-06)
            proj[:, e * HD : (e + 1) * HD] = (numerator * scale).astype(BF16)

    half_inter(h, q_own, pref)
    for c in range(4):
        cols = slice(c * CHUNK, (c + 1) * CHUNK)
        acc[:, cols] = mid[:, cols].astype(F32) + dot(proj[...], wo_v[h, :, cols])
    q_copy.wait()
    half_inter(other, q_other, q_recv)
    stores = []
    for c in range(4):
        cols = slice(c * CHUNK, (c + 1) * CHUNK)
        obuf[:, cols] = (acc[:, cols] + dot(proj[...], wo_v[other, :, cols])).astype(BF16)
        copy = pltpu.make_async_copy(obuf.at[:, cols], out.at[:, cols], load_sem.at[len(loads) + c])
        copy.start()
        stores.append(copy)
    for copy in stores:
        copy.wait()


def shards(sizes, *args):
    ny, nx, nz = sizes
    planes = nx * nz
    piece = HEADS * FEAT // planes
    dma = pltpu.SemaphoreType.DMA
    state = (HEADS, FEAT, HD)
    scratch = [
        pltpu.VMEM((PAD, D), BF16),
        pltpu.VMEM((PAD, D), BF16),
        pltpu.VMEM((8, D, CHUNK), BF16),
        pltpu.VMEM((TAPS, D), F32),
        pltpu.VMEM((D, D), BF16),
        pltpu.VMEM((2, D, HALF), BF16),
        pltpu.VMEM((2, D, HALF), BF16),
        pltpu.VMEM((2, D, HALF), BF16),
        pltpu.VMEM((2, HEADS, HD, FEAT), BF16),
        pltpu.VMEM((2, HALF, D), BF16),
        pltpu.VMEM((2, HEADS, FEAT, HD), BF16),
        pltpu.VMEM((PAD, D), F32),
        pltpu.VMEM((ROWS, D), F32),
        pltpu.VMEM((ROWS, D), BF16),
        pltpu.VMEM((ROWS, D), BF16),
        pltpu.VMEM((ROWS, D), BF16),
        pltpu.VMEM((ROWS, HALF), BF16),
        pltpu.VMEM((2, ROWS, HALF), BF16),
        pltpu.VMEM((2, HEADS, FEAT, ROWS), BF16),
        pltpu.VMEM((2, HEADS, ROWS, HD), F32),
        pltpu.VMEM((2, HEADS, ROWS, FEAT), BF16),
        pltpu.VMEM((ROWS, D), F32),
        pltpu.VMEM((ROWS, D), BF16),
        pltpu.VMEM(state, F32),
        pltpu.VMEM(state, BF16),
        pltpu.VMEM(state, BF16),
        pltpu.VMEM((planes, piece, HD), BF16),
        pltpu.VMEM((planes, piece, HD), BF16),
        pltpu.VMEM((piece, HD), F32),
        pltpu.VMEM((ny, piece, HD), F32),
        pltpu.VMEM((planes, piece, HD), BF16),
        pltpu.VMEM((planes, piece, HD), BF16),
        pltpu.VMEM(state, BF16),
        pltpu.VMEM(state, BF16),
        pltpu.VMEM(state, BF16),
        dma((20,)),
        dma((2,)),
        dma((2,)),
        dma((5,)),
        dma((5,)),
        dma((2,)),
        dma((2,)),
        dma((planes,)),
        dma((planes,)),
        dma((ny,)),
        dma((ny,)),
        dma((planes,)),
        dma((planes,)),
    ]
    return pl.pallas_call(
        functools.partial(kernel, sizes),
        out_shape=jax.ShapeDtypeStruct((ROWS, D), BF16),
        in_specs=[pl.BlockSpec(memory_space=pl.ANY)] * 9,
        out_specs=pl.BlockSpec(memory_space=pl.ANY),
        scratch_shapes=scratch,
        compiler_params=pltpu.CompilerParams(
            collective_id=0, has_side_effects=True, vmem_limit_bytes=60 * 1024 * 1024
        ),
        cost_estimate=pl.CostEstimate(
            flops=10_200_000_000, bytes_accessed=13_000_000, transcendentals=5_000_000
        ),
        name="block",
    )(*args)


def solution(mesh):
    side = round(mesh.shape["tm"] ** (1 / 3))
    sizes = (side, side, side)
    torus = Mesh(mesh.devices.reshape(*sizes, mesh.shape["head"]), AXES)
    rows = P(AXES, None)
    half = P(None, "head")
    in_specs = (rows, P(), P(), P(), half, half, half, P("head", None, None), P("head", None))
    return jax.shard_map(
        functools.partial(shards, sizes), mesh=torus, in_specs=in_specs, out_specs=rows, check_vma=False
    )
```

```python
import functools

import jax
import jax.numpy as jnp
from jax import lax
from jax.experimental import pallas as pl
from jax.experimental.pallas import tpu as pltpu
from jax.sharding import Mesh
from jax.sharding import PartitionSpec as P

AXES = ("tm_0", "tm_1", "tm_2", "head")
MESH = pl.DeviceIdType.MESH
BF16 = jnp.bfloat16
F32 = jnp.float32

ROWS = 512
D = 1024
HALO = 16
PAD = ROWS + 2 * HALO
HALF = 512
HEADS = 4
HD = 128
FEAT = 256
TAPS = 31
CHUNK = 256


def dot(a, b):
    return jnp.dot(a, b, preferred_element_type=F32)


def dot_nt(a, b):
    return lax.dot_general(a, b, (((1,), (1,)), ((), ())), preferred_element_type=F32)


def sigmoid(v):
    return 0.5 * jnp.tanh(0.5 * v) + 0.5


def silu(v):
    half = 0.5 * v
    return half * jnp.tanh(half) + half


def row_stats(read):
    total = read(0)
    for c in range(1, D // 128):
        total = total + read(c)
    mean = jnp.sum(total, axis=-1, keepdims=True) * (1.0 / D)
    spread = None
    for c in range(D // 128):
        center = read(c) - mean
        spread = center * center if spread is None else spread + center * center
    return mean, lax.rsqrt(jnp.sum(spread, axis=-1, keepdims=True) * (1.0 / D) + 1e-05)


def normalize(src, first, dst):
    for i in range(ROWS // 128):
        at = pl.ds(first + i * 128, 128)

        def read(c):
            return src[at, c * 128 : (c + 1) * 128].astype(F32)

        mean, scale = row_stats(read)
        for c in range(D // 128):
            dst[i * 128 : (i + 1) * 128, c * 128 : (c + 1) * 128] = ((read(c) - mean) * scale).astype(BF16)


def gated(c, normed, w_in, glu):
    value = dot(normed[...], w_in[c])
    gate = dot(normed[...], w_in[4 + c])
    glu[HALO : HALO + ROWS, c * CHUNK : (c + 1) * CHUNK] = (
        (value * sigmoid(gate)).astype(BF16).astype(F32)
    )


def convolve(base, count, glu, tap_v, dw):
    for c in range(D // 128):
        cols = slice(c * 128, (c + 1) * 128)
        window = glu[pl.ds(base, count + 32), cols]
        total = None
        for r in range(8):
            part = None
            for q in range(4):
                j = 8 * q + r - 1
                if j < 0:
                    continue
                term = window[8 * q : 8 * q + count + 8] * tap_v[j : j + 1, cols]
                part = term if part is None else part + term
            part = part[r : r + count]
            total = part if total is None else total + part
        dw[pl.ds(base, count), cols] = total


def convolve_inner(glu, tap_v, dw):
    @pl.loop(0, 3)
    def _(i):
        convolve(pl.multiple_of(64 + i * 128, 64), 128, glu, tap_v, dw)


def convolve_edges(glu, tap_v, dw):
    @pl.loop(0, 2)
    def _(i):
        convolve(pl.multiple_of(i * (ROWS - 64), 64), 64, glu, tap_v, dw)


def activate(dw, act):
    for i in range(ROWS // 128):
        at = slice(i * 128, (i + 1) * 128)

        def read(c):
            return dw[at, c * 128 : (c + 1) * 128]

        mean, scale = row_stats(read)
        for c in range(D // 128):
            act[at, c * 128 : (c + 1) * 128] = silu((read(c) - mean) * scale).astype(BF16)


def conv_back(x, act, w_c, mid):
    for c in range(4):
        cols = slice(c * CHUNK, (c + 1) * CHUNK)
        mid[:, cols] = (x[:, cols].astype(F32) + dot(act[...], w_c[:, cols])).astype(BF16)


def key_states(half, c, attn, wk_v, wv_v, fm_v, fmt, proj, val, kmapt, emit):
    wide = slice(c * CHUNK, (c + 1) * CHUNK)
    proj[...] = dot(attn[...], wk_v[half, :, wide]).astype(BF16)
    val[half, :, wide] = dot(attn[...], wv_v[half, :, wide]).astype(BF16)
    for i in range(2):
        e = 2 * c + i
        fmt[half, e] = fm_v[half, e].astype(F32).T.astype(BF16)
        kt = silu(dot_nt(fmt[half, e], proj[:, i * HD : (i + 1) * HD])).astype(BF16)
        kmapt[half, e] = kt
        emit(e, dot(kt, val[half, :, e * HD : (e + 1) * HD]))


def intra(half, c, attn, wq_v, fm_v, proj, qmap, kmapt, val, num):
    side = ROWS // 2
    causal = lax.broadcasted_iota(jnp.int32, (side, side), 0) >= lax.broadcasted_iota(
        jnp.int32, (side, side), 1
    )
    wide = slice(c * CHUNK, (c + 1) * CHUNK)
    proj[...] = dot(attn[...], wq_v[half, :, wide]).astype(BF16)
    for i in range(2):
        e = 2 * c + i
        cols = slice(e * HD, (e + 1) * HD)
        qmap[half, e] = silu(dot(proj[:, i * HD : (i + 1) * HD], fm_v[half, e])).astype(BF16)
        w00 = jnp.where(causal, dot(qmap[half, e, :side], kmapt[half, e, :, :side]), 0.0).astype(BF16)
        num[half, e, :side] = dot(w00, val[half, :side, cols])
        w10 = dot(qmap[half, e, side:], kmapt[half, e, :, :side]).astype(BF16)
        w11 = jnp.where(causal, dot(qmap[half, e, side:], kmapt[half, e, :, side:]), 0.0).astype(BF16)
        num[half, e, side:] = dot(w10, val[half, :side, cols]) + dot(w11, val[half, side:, cols])


def inter(half, e, qmap, prefix, num, attended):
    numerator = num[half, e] + dot(qmap[half, e], prefix[e])
    scale = lax.rsqrt(jnp.mean(numerator * numerator, axis=-1, keepdims=True) + 1e-06)
    attended[:, e * HD : (e + 1) * HD] = (numerator * scale).astype(BF16)


def first_output(half, mid, attended, wo_v, acc):
    for c in range(4):
        cols = slice(c * CHUNK, (c + 1) * CHUNK)
        acc[:, cols] = mid[:, cols].astype(F32) + dot(attended[...], wo_v[half, :, cols])


def last_output(half, acc, attended, wo_v, out):
    for c in range(4):
        cols = slice(c * CHUNK, (c + 1) * CHUNK)
        out[:, cols] = (acc[:, cols] + dot(attended[...], wo_v[half, :, cols])).astype(BF16)


def kernel(
    sizes,
    frames, conv_in, taps, conv_out, wq, wk, wv, fm, wo, out,
    x_v, normed, w_in, tap_v, w_c, wq_v, wk_v, wv_v, fm_v, wo_v, fmt,
    glu, dw, act, mid, attn, proj, val, kmapt, num, qmap, acc, attended,
    st_own, p_send, p_recv, a_send, a_recv, y_send, y_recv, r_send, r_recv, pref, q_send, q_recv,
    load_sem, halo_s, halo_r, w_s, w_r, p_s, p_r, a_s, a_r, y_s, y_r, r_s, r_r, q_s, q_r,
):
    ny, nx, nz = sizes
    planes = nx * nz
    count = ny * planes * 2
    y, x, z, h = [lax.axis_index(a) for a in AXES]
    plane = x * nz + z
    lin = ((y * nx + x) * nz + z) * 2 + h
    other = 1 - h
    pair = (y, x, z, other)
    has_prev = lin > 0
    has_next = lin < count - 1

    def device(n):
        chip = lax.div(n, 2)
        column = lax.rem(chip, planes)
        return (lax.div(chip, planes), lax.div(column, nz), lax.rem(column, nz), lax.rem(n, 2))

    prev = device(lax.rem(lin + count - 1, count))
    following = device(lax.rem(lin + 1, count))

    def plane_peer(k):
        p = lax.rem(plane + k, planes)
        return (y, lax.div(p, nz), lax.rem(p, nz), h)

    loads = []

    def load(src, dst):
        copy = pltpu.make_async_copy(src, dst, load_sem.at[len(loads)])
        copy.start()
        loads.append(copy)
        return copy

    ld_x = load(frames, x_v)
    ld_in = []
    for c in range(8):
        at = (c % 2) * 4 + c // 2
        ld_in.append(load(conv_in.at[:, pl.ds(at * CHUNK, CHUNK)], w_in.at[at]))
    ld_tap = load(taps, tap_v)
    ld_c = load(conv_out, w_c)
    ld_k = load(wk, wk_v.at[h])
    ld_v = load(wv, wv_v.at[h])
    ld_f = load(fm, fm_v.at[h])
    ld_q = load(wq, wq_v.at[h])
    ld_o = load(wo, wo_v.at[h])

    barrier = pltpu.get_barrier_semaphore()

    def greet(d):
        pl.semaphore_signal(barrier, inc=1, device_id=d, device_id_type=MESH)

    @pl.when(has_prev)
    def _():
        greet(prev)

    @pl.when(has_next)
    def _():
        greet(following)

    greet(pair)

    @pl.loop(1, planes)
    def _(k):
        greet(plane_peer(k))

    for k in range(1, ny):
        greet((lax.rem(y + k, ny), x, z, h))

    def remote(src, dst, s, r, d):
        return pltpu.make_async_remote_copy(
            src_ref=src, dst_ref=dst, send_sem=s, recv_sem=r, device_id=d, device_id_type=MESH
        )

    ld_x.wait()
    normalize(x_v, 0, normed)
    for c in range(4):
        ld_in[2 * c].wait()
        ld_in[2 * c + 1].wait()
        gated(c, normed, w_in, glu)

    pl.semaphore_wait(
        barrier, 1 + planes - 1 + ny - 1 + has_prev.astype(jnp.int32) + has_next.astype(jnp.int32)
    )
    low = remote(
        glu.at[pl.ds(HALO, HALO)], glu.at[pl.ds(HALO + ROWS, HALO)], halo_s.at[0], halo_r.at[0], prev
    )
    high = remote(
        glu.at[pl.ds(ROWS, HALO)], glu.at[pl.ds(0, HALO)], halo_s.at[1], halo_r.at[1], following
    )

    @pl.when(has_prev)
    def _():
        low.start()

    @pl.when(has_next)
    def _():
        high.start()

    weights = []
    for i, (src, dst) in enumerate(((wk, wk_v), (wv, wv_v), (fm, fm_v), (wq, wq_v), (wo, wo_v))):
        copy = remote(src, dst.at[h], w_s.at[i], w_r.at[i], pair)
        copy.start()
        weights.append(copy)

    ld_tap.wait()
    convolve_inner(glu, tap_v, dw)

    @pl.when(has_prev)
    def _():
        low.wait_send()
        high.wait_recv()

    @pl.when(has_next)
    def _():
        high.wait_send()
        low.wait_recv()

    @pl.when(jnp.logical_not(has_prev))
    def _():
        glu[pl.ds(0, HALO), :] = jnp.zeros((HALO, D), F32)

    @pl.when(jnp.logical_not(has_next))
    def _():
        glu[pl.ds(HALO + ROWS, HALO), :] = jnp.zeros((HALO, D), F32)

    convolve_edges(glu, tap_v, dw)
    activate(dw, act)

    ld_c.wait()
    conv_back(x_v, act, w_c, mid)
    normalize(mid, 0, attn)

    ld_k.wait()
    ld_v.wait()
    ld_f.wait()
    for copy in weights[:3]:
        copy.wait()

    def emit_other(e, s):
        p_send[e] = s.astype(BF16)

    def emit_own(e, s):
        st_own[e] = s

    def keys(half, c, emit):
        key_states(half, c, attn, wk_v, wv_v, fm_v, fmt, proj, val, kmapt, emit)

    def queries(half, c):
        intra(half, c, attn, wq_v, fm_v, proj, qmap, kmapt, val, num)

    piece = 2 * FEAT // planes
    per = planes // 2

    def p_copy(c):
        at = pl.ds(2 * c, 2)
        return remote(p_send.at[at], p_recv.at[at], p_s.at[c], p_r.at[c], pair)

    def q_copy(c):
        at = pl.ds(2 * c, 2)
        return remote(q_send.at[at], q_recv.at[at], q_s.at[c], q_r.at[c], pair)

    def a_copy(c, k):
        p = lax.rem(plane + k, planes)
        return remote(a_send.at[c, p], a_recv.at[c, plane], a_s.at[c, k], a_r.at[c, k], plane_peer(k))

    def r_copy(c, k):
        p = lax.rem(plane + k, planes)
        return remote(r_send.at[c, p], r_recv.at[c, plane], r_s.at[c, k], r_r.at[c, k], plane_peer(k))

    def y_copy(c, k):
        return remote(
            y_send.at[c], y_recv.at[c, k], y_s.at[c, k], y_r.at[c, k], (lax.rem(y + k, ny), x, z, h)
        )

    def a_start(c):
        p_copy(c).wait()
        for i in range(2):
            e = 2 * c + i
            chip_state = (st_own[e] + p_recv[e].astype(F32)).astype(BF16)
            a_send[c, i * per : (i + 1) * per] = chip_state.reshape(per, piece, HD)

        @pl.loop(1, planes)
        def _(k):
            a_copy(c, k).start()

        a_recv[c, plane] = a_send[c, plane]

    def y_start(c):
        @pl.loop(1, planes)
        def _(k):
            a_copy(c, k).wait()

        run = a_recv[c, 0].astype(F32)
        for p in range(1, planes):
            run = run + a_recv[c, p].astype(F32)
        y_send[c] = run
        for k in range(1, ny):

            @pl.when(y + k < ny)
            def _():
                y_copy(c, k).start()

    def r_start(c):
        for k in range(1, ny):

            @pl.when(y + k < ny)
            def _():
                y_copy(c, k).wait_send()

            @pl.when(y >= k)
            def _():
                y_copy(c, k).wait_recv()

        run = jnp.zeros((piece, HD), F32)
        for k in range(1, ny):
            run = run + jnp.where(y >= k, y_recv[c, k], 0.0)
        for p in range(planes):
            r_send[c, p] = run.astype(BF16)
            run = run + a_recv[c, p].astype(F32)

        @pl.loop(1, planes)
        def _(k):
            r_copy(c, k).start()

        r_recv[c, plane] = r_send[c, plane]

    def q_start(c):
        @pl.loop(1, planes)
        def _(k):
            r_copy(c, k).wait()

        for i in range(2):
            e = 2 * c + i
            before = r_recv[c, i * per : (i + 1) * per].reshape(FEAT, HD).astype(F32)
            q_send[e] = (before + jnp.where(h == 0, st_own[e], 0.0)).astype(BF16)
            pref[e] = (before + jnp.where(h == 1, p_recv[e].astype(F32), 0.0)).astype(BF16)
        q_copy(c).start()

    keys(other, 0, emit_other)
    p_copy(0).start()
    keys(other, 1, emit_other)
    p_copy(1).start()
    keys(h, 0, emit_own)
    a_start(0)
    keys(h, 1, emit_own)
    a_start(1)
    ld_q.wait()
    ld_o.wait()
    weights[3].wait()
    weights[4].wait()
    queries(other, 0)
    y_start(0)
    queries(other, 1)
    y_start(1)
    r_start(0)
    queries(h, 0)
    r_start(1)
    queries(h, 1)
    q_start(0)
    inter(h, 0, qmap, pref, num, attended)
    inter(h, 1, qmap, pref, num, attended)
    q_start(1)
    inter(h, 2, qmap, pref, num, attended)
    inter(h, 3, qmap, pref, num, attended)
    first_output(h, mid, attended, wo_v, acc)
    for c in range(2):
        q_copy(c).wait()
        for i in range(2):
            inter(other, 2 * c + i, qmap, q_recv, num, attended)
    last_output(other, acc, attended, wo_v, out)


def shards(sizes, *args):
    ny, nx, nz = sizes
    planes = nx * nz
    piece = 2 * FEAT // planes
    dma = pltpu.SemaphoreType.DMA
    state = (HEADS, FEAT, HD)
    scratch = [
        pltpu.VMEM((ROWS, D), BF16),
        pltpu.VMEM((ROWS, D), BF16),
        pltpu.VMEM((8, D, CHUNK), BF16),
        pltpu.VMEM((TAPS, D), F32),
        pltpu.VMEM((D, D), BF16),
        pltpu.VMEM((2, D, HALF), BF16),
        pltpu.VMEM((2, D, HALF), BF16),
        pltpu.VMEM((2, D, HALF), BF16),
        pltpu.VMEM((2, HEADS, HD, FEAT), BF16),
        pltpu.VMEM((2, HALF, D), BF16),
        pltpu.VMEM((2, HEADS, FEAT, HD), BF16),
        pltpu.VMEM((PAD, D), F32),
        pltpu.VMEM((ROWS, D), F32),
        pltpu.VMEM((ROWS, D), BF16),
        pltpu.VMEM((ROWS, D), BF16),
        pltpu.VMEM((ROWS, D), BF16),
        pltpu.VMEM((ROWS, CHUNK), BF16),
        pltpu.VMEM((2, ROWS, HALF), BF16),
        pltpu.VMEM((2, HEADS, FEAT, ROWS), BF16),
        pltpu.VMEM((2, HEADS, ROWS, HD), F32),
        pltpu.VMEM((2, HEADS, ROWS, FEAT), BF16),
        pltpu.VMEM((ROWS, D), F32),
        pltpu.VMEM((ROWS, HALF), BF16),
        pltpu.VMEM(state, F32),
        pltpu.VMEM(state, BF16),
        pltpu.VMEM(state, BF16),
        pltpu.VMEM((2, planes, piece, HD), BF16),
        pltpu.VMEM((2, planes, piece, HD), BF16),
        pltpu.VMEM((2, piece, HD), F32),
        pltpu.VMEM((2, ny, piece, HD), F32),
        pltpu.VMEM((2, planes, piece, HD), BF16),
        pltpu.VMEM((2, planes, piece, HD), BF16),
        pltpu.VMEM(state, BF16),
        pltpu.VMEM(state, BF16),
        pltpu.VMEM(state, BF16),
        dma((16,)),
        dma((2,)),
        dma((2,)),
        dma((5,)),
        dma((5,)),
        dma((2,)),
        dma((2,)),
        dma((2, planes)),
        dma((2, planes)),
        dma((2, ny)),
        dma((2, ny)),
        dma((2, planes)),
        dma((2, planes)),
        dma((2,)),
        dma((2,)),
    ]
    return pl.pallas_call(
        functools.partial(kernel, sizes),
        out_shape=pltpu.VMEM((ROWS, D), BF16),
        in_specs=[pl.BlockSpec(memory_space=pl.ANY)] * 9,
        out_specs=pl.BlockSpec(memory_space=pltpu.VMEM),
        scratch_shapes=scratch,
        compiler_params=pltpu.CompilerParams(
            collective_id=0, has_side_effects=True, vmem_limit_bytes=56 * 1024 * 1024
        ),
        cost_estimate=pl.CostEstimate(
            flops=10_200_000_000, bytes_accessed=13_000_000, transcendentals=5_000_000
        ),
        name="block",
    )(*args)


def solution(mesh):
    side = round(mesh.shape["tm"] ** (1 / 3))
    sizes = (side, side, side)
    torus = Mesh(mesh.devices.reshape(*sizes, mesh.shape["head"]), AXES)
    rows = P(AXES, None)
    half = P(None, "head")
    in_specs = (rows, P(), P(), P(), half, half, half, P("head", None, None), P("head", None))
    return jax.shard_map(
        functools.partial(shards, sizes), mesh=torus, in_specs=in_specs, out_specs=rows, check_vma=False
    )
```

```python
import functools

import jax
import jax.numpy as jnp
from jax import lax
from jax.experimental import pallas as pl
from jax.experimental.pallas import tpu as pltpu
from jax.sharding import Mesh
from jax.sharding import PartitionSpec as P

AXES = ("tm_0", "tm_1", "tm_2", "head")
MESH = pl.DeviceIdType.MESH
BF16 = jnp.bfloat16
F32 = jnp.float32

ROWS = 512
D = 1024
HALO = 16
PAD = ROWS + 2 * HALO
HALF = 512
HEADS = 4
HD = 128
FEAT = 256
TAPS = 31
CHUNK = 256


def dot(a, b):
    return jnp.dot(a, b, preferred_element_type=F32)


def dot_nt(a, b):
    return lax.dot_general(a, b, (((1,), (1,)), ((), ())), preferred_element_type=F32)


def sigmoid(v):
    return 0.5 * jnp.tanh(0.5 * v) + 0.5


def silu(v):
    half = 0.5 * v
    return half * jnp.tanh(half) + half


def row_stats(read):
    total = read(0)
    for c in range(1, D // 128):
        total = total + read(c)
    mean = jnp.sum(total, axis=-1, keepdims=True) * (1.0 / D)
    spread = None
    for c in range(D // 128):
        center = read(c) - mean
        spread = center * center if spread is None else spread + center * center
    return mean, lax.rsqrt(jnp.sum(spread, axis=-1, keepdims=True) * (1.0 / D) + 1e-05)


def normalize(src, first, last, dst):
    for i in range(first, last):
        at = pl.ds(i * 128, 128)

        def read(c):
            return src[at, c * 128 : (c + 1) * 128].astype(F32)

        mean, scale = row_stats(read)
        for c in range(D // 128):
            dst[i * 128 : (i + 1) * 128, c * 128 : (c + 1) * 128] = ((read(c) - mean) * scale).astype(BF16)


def gated(c, normed, w_in, glu):
    value = dot(normed[...], w_in[c])
    gate = dot(normed[...], w_in[4 + c])
    glu[HALO : HALO + ROWS, c * CHUNK : (c + 1) * CHUNK] = (
        (value * sigmoid(gate)).astype(BF16).astype(F32)
    )


def convolve(base, count, glu, tap_v, dw):
    for c in range(D // 128):
        cols = slice(c * 128, (c + 1) * 128)
        window = glu[pl.ds(base, count + 32), cols]
        total = None
        for r in range(8):
            part = None
            for q in range(4):
                j = 8 * q + r - 1
                if j < 0:
                    continue
                term = window[8 * q : 8 * q + count + 8] * tap_v[j : j + 1, cols]
                part = term if part is None else part + term
            part = part[r : r + count]
            total = part if total is None else total + part
        dw[pl.ds(base, count), cols] = total


def convolve_inner(glu, tap_v, dw):
    @pl.loop(0, 3)
    def _(i):
        convolve(pl.multiple_of(64 + i * 128, 64), 128, glu, tap_v, dw)


def convolve_edges(glu, tap_v, dw):
    @pl.loop(0, 2)
    def _(i):
        convolve(pl.multiple_of(i * (ROWS - 64), 64), 64, glu, tap_v, dw)


def activate(dw, act):
    for i in range(ROWS // 128):
        at = slice(i * 128, (i + 1) * 128)

        def read(c):
            return dw[at, c * 128 : (c + 1) * 128]

        mean, scale = row_stats(read)
        for c in range(D // 128):
            act[at, c * 128 : (c + 1) * 128] = silu((read(c) - mean) * scale).astype(BF16)


def conv_back(x, act, w_c, mid):
    for c in range(4):
        cols = slice(c * CHUNK, (c + 1) * CHUNK)
        mid[:, cols] = (x[:, cols].astype(F32) + dot(act[...], w_c[:, cols])).astype(BF16)


def key_states(half, c, attn, wk_v, wv_v, fmt, val, kmapt, emit):
    wide = slice(c * CHUNK, (c + 1) * CHUNK)
    key = dot(attn[...], wk_v[half, :, wide]).astype(BF16)
    value = dot(attn[...], wv_v[half, :, wide]).astype(BF16)
    val[half, :, wide] = value
    maps = [dot_nt(fmt[half, 2 * c + i], key[:, i * HD : (i + 1) * HD]) for i in range(2)]
    maps = [silu(m).astype(BF16) for m in maps]
    for i in range(2):
        kmapt[half, 2 * c + i] = maps[i]
        emit(2 * c + i, dot(maps[i], value[:, i * HD : (i + 1) * HD]))


def intra(half, c, attn, wq_v, fm_v, proj, qmap, kmapt, val, num):
    side = ROWS // 2
    causal = lax.broadcasted_iota(jnp.int32, (side, side), 0) >= lax.broadcasted_iota(
        jnp.int32, (side, side), 1
    )
    wide = slice(c * CHUNK, (c + 1) * CHUNK)
    proj[...] = dot(attn[...], wq_v[half, :, wide]).astype(BF16)
    for i in range(2):
        e = 2 * c + i
        cols = slice(e * HD, (e + 1) * HD)
        qmap[half, e] = silu(dot(proj[:, i * HD : (i + 1) * HD], fm_v[half, e])).astype(BF16)
        w00 = jnp.where(causal, dot(qmap[half, e, :side], kmapt[half, e, :, :side]), 0.0).astype(BF16)
        num[half, e, :side] = dot(w00, val[half, :side, cols])
        w10 = dot(qmap[half, e, side:], kmapt[half, e, :, :side]).astype(BF16)
        w11 = jnp.where(causal, dot(qmap[half, e, side:], kmapt[half, e, :, side:]), 0.0).astype(BF16)
        num[half, e, side:] = dot(w10, val[half, :side, cols]) + dot(w11, val[half, side:, cols])


def inter(half, e, qmap, prefix, num, attended):
    numerator = num[half, e] + dot(qmap[half, e], prefix[e])
    scale = lax.rsqrt(jnp.mean(numerator * numerator, axis=-1, keepdims=True) + 1e-06)
    attended[half, :, e * HD : (e + 1) * HD] = (numerator * scale).astype(BF16)


def out_part(half, heads, cols, attended, wo_v):
    part = slice(heads * CHUNK, (heads + 1) * CHUNK)
    return dot(attended[half, :, part], wo_v[half, part, cols])


def first_output(mid, attended, wo_v, acc):
    for c in range(4):
        cols = slice(c * CHUNK, (c + 1) * CHUNK)
        both = out_part(0, 0, cols, attended, wo_v) + out_part(1, 0, cols, attended, wo_v)
        acc[:, cols] = mid[:, cols].astype(F32) + both


def own_output(own, attended, wo_v, acc):
    for c in range(4):
        cols = slice(c * CHUNK, (c + 1) * CHUNK)
        acc[:, cols] += out_part(own, 1, cols, attended, wo_v)


def last_output(other, attended, wo_v, acc, out):
    for c in range(4):
        cols = slice(c * CHUNK, (c + 1) * CHUNK)
        out[:, cols] = (acc[:, cols] + out_part(other, 1, cols, attended, wo_v)).astype(BF16)


def kernel(
    sizes,
    frames, conv_in, taps, conv_out, wq, wk, wv, fm, wo, out,
    x_v, normed, w_in, tap_v, w_c, wq_v, wk_v, wv_v, fm_v, wo_v, fmt,
    glu, dw, act, mid, attn, proj, val, kmapt, num, qmap, acc, attended,
    st_own, p_send, p_recv, a_send, a_recv, y_send, y_recv, r_send, r_recv, pref, q_send, q_recv,
    load_sem, halo_s, halo_r, w_s, w_r, p_s, p_r, a_s, a_r, y_s, y_r, r_s, r_r, q_s, q_r,
):
    ny, nx, nz = sizes
    planes = nx * nz
    count = ny * planes * 2
    y, x, z, h = [lax.axis_index(a) for a in AXES]
    plane = x * nz + z
    lin = ((y * nx + x) * nz + z) * 2 + h
    other, own = 0, 1
    pair = (y, x, z, 1 - h)
    has_prev = lin > 0
    has_next = lin < count - 1

    def device(n):
        chip = lax.div(n, 2)
        column = lax.rem(chip, planes)
        return (lax.div(chip, planes), lax.div(column, nz), lax.rem(column, nz), lax.rem(n, 2))

    prev = device(lax.rem(lin + count - 1, count))
    following = device(lax.rem(lin + 1, count))

    def plane_peer(k):
        p = lax.rem(plane + k, planes)
        return (y, lax.div(p, nz), lax.rem(p, nz), h)

    loads = []

    def load(src, dst):
        copy = pltpu.make_async_copy(src, dst, load_sem.at[len(loads)])
        copy.start()
        loads.append(copy)
        return copy

    ld_x = []
    for at in (pl.ds(0, ROWS // 2), pl.ds(ROWS // 2, ROWS // 2)):
        ld_x.append(load(frames.at[at], x_v.at[at]))
    ld_f = load(fm, fm_v.at[own])
    ld_in = []
    for c in range(8):
        at = (c % 2) * 4 + c // 2
        ld_in.append(load(conv_in.at[:, pl.ds(at * CHUNK, CHUNK)], w_in.at[at]))
    barrier = pltpu.get_barrier_semaphore()

    def greet(d):
        pl.semaphore_signal(barrier, inc=1, device_id=d, device_id_type=MESH)

    @pl.when(has_prev)
    def _():
        greet(prev)

    @pl.when(has_next)
    def _():
        greet(following)

    greet(pair)

    @pl.loop(1, planes)
    def _(k):
        greet(plane_peer(k))

    for k in range(1, ny):
        greet((lax.rem(y + k, ny), x, z, h))

    def remote(src, dst, s, r, d):
        return pltpu.make_async_remote_copy(
            src_ref=src, dst_ref=dst, send_sem=s, recv_sem=r, device_id=d, device_id_type=MESH
        )

    ld_x[0].wait()
    ld_tap = load(taps, tap_v)
    ld_c = load(conv_out, w_c)
    ld_k = load(wk, wk_v.at[own])
    ld_v = load(wv, wv_v.at[own])
    ld_q = load(wq, wq_v.at[own])
    ld_o = load(wo, wo_v.at[own])
    normalize(x_v, 0, 2, normed)
    ld_x[1].wait()
    normalize(x_v, 2, 4, normed)
    ld_f.wait()
    for e in range(HEADS):
        fmt[own, e] = fm_v[own, e].astype(F32).T.astype(BF16)
    for c in range(4):
        ld_in[2 * c].wait()
        ld_in[2 * c + 1].wait()
        gated(c, normed, w_in, glu)

    pl.semaphore_wait(
        barrier, 1 + planes - 1 + ny - 1 + has_prev.astype(jnp.int32) + has_next.astype(jnp.int32)
    )
    low = remote(
        glu.at[pl.ds(HALO, HALO)], glu.at[pl.ds(HALO + ROWS, HALO)], halo_s.at[0], halo_r.at[0], prev
    )
    high = remote(
        glu.at[pl.ds(ROWS, HALO)], glu.at[pl.ds(0, HALO)], halo_s.at[1], halo_r.at[1], following
    )

    @pl.when(has_prev)
    def _():
        low.start()

    @pl.when(has_next)
    def _():
        high.start()

    weights = []
    for i, (src, dst) in enumerate(((wk, wk_v), (wv, wv_v), (fmt.at[own], fmt), (fm, fm_v), (wq, wq_v), (wo, wo_v))):
        copy = remote(src, dst.at[other], w_s.at[i], w_r.at[i], pair)
        copy.start()
        weights.append(copy)

    ld_tap.wait()
    convolve_inner(glu, tap_v, dw)

    @pl.when(has_prev)
    def _():
        low.wait_send()
        high.wait_recv()

    @pl.when(has_next)
    def _():
        high.wait_send()
        low.wait_recv()

    @pl.when(jnp.logical_not(has_prev))
    def _():
        glu[pl.ds(0, HALO), :] = jnp.zeros((HALO, D), F32)

    @pl.when(jnp.logical_not(has_next))
    def _():
        glu[pl.ds(HALO + ROWS, HALO), :] = jnp.zeros((HALO, D), F32)

    convolve_edges(glu, tap_v, dw)
    activate(dw, act)

    ld_c.wait()
    conv_back(x_v, act, w_c, mid)
    normalize(mid, 0, ROWS // 128, attn)

    ld_k.wait()
    ld_v.wait()
    for copy in weights[:3]:
        copy.wait()

    def emit_other(e, s):
        p_send[e] = s.astype(BF16)

    def emit_own(e, s):
        st_own[e] = s

    def keys(half, c, emit):
        key_states(half, c, attn, wk_v, wv_v, fmt, val, kmapt, emit)

    def queries(half, c):
        intra(half, c, attn, wq_v, fm_v, proj, qmap, kmapt, val, num)

    piece = 2 * FEAT // planes
    per = planes // 2

    def p_copy(c):
        at = pl.ds(2 * c, 2)
        return remote(p_send.at[at], p_recv.at[at], p_s.at[c], p_r.at[c], pair)

    def q_copy(c):
        at = pl.ds(2 * c, 2)
        return remote(q_send.at[at], q_recv.at[at], q_s.at[c], q_r.at[c], pair)

    def a_copy(c, k):
        p = lax.rem(plane + k, planes)
        return remote(a_send.at[c, p], a_recv.at[c, plane], a_s.at[c, k], a_r.at[c, k], plane_peer(k))

    def r_copy(c, k):
        p = lax.rem(plane + k, planes)
        return remote(r_send.at[c, p], r_recv.at[c, plane], r_s.at[c, k], r_r.at[c, k], plane_peer(k))

    def y_copy(c, k):
        return remote(
            y_send.at[c], y_recv.at[c, k], y_s.at[c, k], y_r.at[c, k], (lax.rem(y + k, ny), x, z, h)
        )

    def a_start(c):
        p_copy(c).wait()
        for i in range(2):
            e = 2 * c + i
            chip_state = (st_own[e] + p_recv[e].astype(F32)).astype(BF16)
            a_send[c, i * per : (i + 1) * per] = chip_state.reshape(per, piece, HD)

        @pl.loop(1, planes, unroll=True)
        def _(k):
            a_copy(c, k).start()

        a_recv[c, plane] = a_send[c, plane]

    def y_start(c):
        @pl.loop(1, planes, unroll=True)
        def _(k):
            a_copy(c, k).wait()

        run = a_recv[c, 0].astype(F32)
        for p in range(1, planes):
            run = run + a_recv[c, p].astype(F32)
        y_send[c] = run
        for k in range(1, ny):

            @pl.when(y + k < ny)
            def _():
                y_copy(c, k).start()

    def r_start(c):
        for k in range(1, ny):

            @pl.when(y + k < ny)
            def _():
                y_copy(c, k).wait_send()

            @pl.when(y >= k)
            def _():
                y_copy(c, k).wait_recv()

        run = jnp.zeros((piece, HD), F32)
        for k in range(1, ny):
            run = run + jnp.where(y >= k, y_recv[c, k], 0.0)
        for p in range(planes):
            r_send[c, p] = run.astype(BF16)
            run = run + a_recv[c, p].astype(F32)

        @pl.loop(1, planes, unroll=True)
        def _(k):
            r_copy(c, k).start()

        r_recv[c, plane] = r_send[c, plane]

    def q_start(c):
        @pl.loop(1, planes, unroll=True)
        def _(k):
            r_copy(c, k).wait()

        for i in range(2):
            e = 2 * c + i
            before = r_recv[c, i * per : (i + 1) * per].reshape(FEAT, HD).astype(F32)
            q_send[e] = (before + jnp.where(h == 0, st_own[e], 0.0)).astype(BF16)
            pref[e] = (before + jnp.where(h == 1, p_recv[e].astype(F32), 0.0)).astype(BF16)
        q_copy(c).start()

    keys(other, 0, emit_other)
    p_copy(0).start()
    keys(own, 0, emit_own)
    a_start(0)
    keys(other, 1, emit_other)
    p_copy(1).start()
    keys(own, 1, emit_own)
    a_start(1)
    ld_q.wait()
    ld_o.wait()
    for copy in weights[3:]:
        copy.wait()
    queries(other, 0)
    y_start(0)
    queries(other, 1)
    y_start(1)
    r_start(0)
    queries(own, 0)
    r_start(1)
    queries(own, 1)
    q_start(0)
    inter(own, 0, qmap, pref, num, attended)
    inter(own, 1, qmap, pref, num, attended)
    q_copy(0).wait()
    inter(other, 0, qmap, q_recv, num, attended)
    inter(other, 1, qmap, q_recv, num, attended)
    first_output(mid, attended, wo_v, acc)
    q_start(1)
    inter(own, 2, qmap, pref, num, attended)
    inter(own, 3, qmap, pref, num, attended)
    own_output(own, attended, wo_v, acc)
    q_copy(1).wait()
    inter(other, 2, qmap, q_recv, num, attended)
    inter(other, 3, qmap, q_recv, num, attended)
    last_output(other, attended, wo_v, acc, out)


def shards(sizes, *args):
    ny, nx, nz = sizes
    planes = nx * nz
    piece = 2 * FEAT // planes
    dma = pltpu.SemaphoreType.DMA
    state = (HEADS, FEAT, HD)
    scratch = [
        pltpu.VMEM((ROWS, D), BF16),
        pltpu.VMEM((ROWS, D), BF16),
        pltpu.VMEM((8, D, CHUNK), BF16),
        pltpu.VMEM((TAPS, D), F32),
        pltpu.VMEM((D, D), BF16),
        pltpu.VMEM((2, D, HALF), BF16),
        pltpu.VMEM((2, D, HALF), BF16),
        pltpu.VMEM((2, D, HALF), BF16),
        pltpu.VMEM((2, HEADS, HD, FEAT), BF16),
        pltpu.VMEM((2, HALF, D), BF16),
        pltpu.VMEM((2, HEADS, FEAT, HD), BF16),
        pltpu.VMEM((PAD, D), F32),
        pltpu.VMEM((ROWS, D), F32),
        pltpu.VMEM((ROWS, D), BF16),
        pltpu.VMEM((ROWS, D), BF16),
        pltpu.VMEM((ROWS, D), BF16),
        pltpu.VMEM((ROWS, CHUNK), BF16),
        pltpu.VMEM((2, ROWS, HALF), BF16),
        pltpu.VMEM((2, HEADS, FEAT, ROWS), BF16),
        pltpu.VMEM((2, HEADS, ROWS, HD), F32),
        pltpu.VMEM((2, HEADS, ROWS, FEAT), BF16),
        pltpu.VMEM((ROWS, D), F32),
        pltpu.VMEM((2, ROWS, HALF), BF16),
        pltpu.VMEM(state, F32),
        pltpu.VMEM(state, BF16),
        pltpu.VMEM(state, BF16),
        pltpu.VMEM((2, planes, piece, HD), BF16),
        pltpu.VMEM((2, planes, piece, HD), BF16),
        pltpu.VMEM((2, piece, HD), F32),
        pltpu.VMEM((2, ny, piece, HD), F32),
        pltpu.VMEM((2, planes, piece, HD), BF16),
        pltpu.VMEM((2, planes, piece, HD), BF16),
        pltpu.VMEM(state, BF16),
        pltpu.VMEM(state, BF16),
        pltpu.VMEM(state, BF16),
        dma((17,)),
        dma((2,)),
        dma((2,)),
        dma((6,)),
        dma((6,)),
        dma((2,)),
        dma((2,)),
        dma((2, planes)),
        dma((2, planes)),
        dma((2, ny)),
        dma((2, ny)),
        dma((2, planes)),
        dma((2, planes)),
        dma((2,)),
        dma((2,)),
    ]
    return pl.pallas_call(
        functools.partial(kernel, sizes),
        out_shape=pltpu.VMEM((ROWS, D), BF16),
        in_specs=[pl.BlockSpec(memory_space=pl.ANY)] * 9,
        out_specs=pl.BlockSpec(memory_space=pltpu.VMEM),
        scratch_shapes=scratch,
        compiler_params=pltpu.CompilerParams(
            collective_id=0, has_side_effects=True, vmem_limit_bytes=56 * 1024 * 1024
        ),
        cost_estimate=pl.CostEstimate(
            flops=10_200_000_000, bytes_accessed=13_000_000, transcendentals=5_000_000
        ),
        name="block",
    )(*args)


def solution(mesh):
    side = round(mesh.shape["tm"] ** (1 / 3))
    sizes = (side, side, side)
    torus = Mesh(mesh.devices.reshape(*sizes, mesh.shape["head"]), AXES)
    rows = P(AXES, None)
    half = P(None, "head")
    in_specs = (rows, P(), P(), P(), half, half, half, P("head", None, None), P("head", None))
    return jax.shard_map(
        functools.partial(shards, sizes), mesh=torus, in_specs=in_specs, out_specs=rows, check_vma=False
    )
```

```python
import functools

import jax
import jax.numpy as jnp
from jax import lax
from jax.experimental import pallas as pl
from jax.experimental.pallas import tpu as pltpu
from jax.sharding import Mesh
from jax.sharding import PartitionSpec as P

AXES = ("tm_0", "tm_1", "tm_2", "head")
MESH = pl.DeviceIdType.MESH
BF16 = jnp.bfloat16
F32 = jnp.float32

ROWS = 512
D = 1024
HALO = 16
PAD = ROWS + 2 * HALO
HALF = 512
HEADS = 4
HD = 128
FEAT = 256
TAPS = 31
CHUNK = 256


def dot(a, b):
    return jnp.dot(a, b, preferred_element_type=F32)


def dot_nt(a, b):
    return lax.dot_general(a, b, (((1,), (1,)), ((), ())), preferred_element_type=F32)


def sigmoid(v):
    return 0.5 * jnp.tanh(0.5 * v) + 0.5


def silu(v):
    half = 0.5 * v
    return half * jnp.tanh(half) + half


def row_stats(read):
    total = read(0)
    for c in range(1, D // 128):
        total = total + read(c)
    mean = jnp.sum(total, axis=-1, keepdims=True) * (1.0 / D)
    spread = None
    for c in range(D // 128):
        center = read(c) - mean
        spread = center * center if spread is None else spread + center * center
    return mean, lax.rsqrt(jnp.sum(spread, axis=-1, keepdims=True) * (1.0 / D) + 1e-05)


def normalize(src, first, last, dst):
    for i in range(first, last):
        at = pl.ds(i * 128, 128)

        def read(c):
            return src[at, c * 128 : (c + 1) * 128].astype(F32)

        mean, scale = row_stats(read)
        for c in range(D // 128):
            dst[i * 128 : (i + 1) * 128, c * 128 : (c + 1) * 128] = ((read(c) - mean) * scale).astype(BF16)


def gated(c, normed, w_in, glu):
    value = dot(normed[...], w_in[c])
    gate = dot(normed[...], w_in[4 + c])
    glu[HALO : HALO + ROWS, c * CHUNK : (c + 1) * CHUNK] = (
        (value * sigmoid(gate)).astype(BF16).astype(F32)
    )


def convolve(base, count, glu, tap_v, dw):
    for c in range(D // 128):
        cols = slice(c * 128, (c + 1) * 128)
        window = glu[pl.ds(base, count + 32), cols]
        total = None
        for r in range(8):
            part = None
            for q in range(4):
                j = 8 * q + r - 1
                if j < 0:
                    continue
                term = window[8 * q : 8 * q + count + 8] * tap_v[j : j + 1, cols]
                part = term if part is None else part + term
            part = part[r : r + count]
            total = part if total is None else total + part
        dw[pl.ds(base, count), cols] = total


def convolve_inner(glu, tap_v, dw):
    @pl.loop(0, 3)
    def _(i):
        convolve(pl.multiple_of(64 + i * 128, 64), 128, glu, tap_v, dw)


def convolve_edges(glu, tap_v, dw):
    @pl.loop(0, 2)
    def _(i):
        convolve(pl.multiple_of(i * (ROWS - 64), 64), 64, glu, tap_v, dw)


def activate(dw, act):
    for i in range(ROWS // 128):
        at = slice(i * 128, (i + 1) * 128)

        def read(c):
            return dw[at, c * 128 : (c + 1) * 128]

        mean, scale = row_stats(read)
        for c in range(D // 128):
            act[at, c * 128 : (c + 1) * 128] = silu((read(c) - mean) * scale).astype(BF16)


def conv_back(x, act, w_c, mid):
    for c in range(4):
        cols = slice(c * CHUNK, (c + 1) * CHUNK)
        mid[:, cols] = (x[:, cols].astype(F32) + dot(act[...], w_c[:, cols])).astype(BF16)


def key_states(half, c, attn, wk_v, wv_v, fmt, val, kmapt, emit):
    wide = slice(c * CHUNK, (c + 1) * CHUNK)
    key = dot(attn[...], wk_v[half, :, wide]).astype(BF16)
    value = dot(attn[...], wv_v[half, :, wide]).astype(BF16)
    val[half, :, wide] = value
    maps = [dot_nt(fmt[half, 2 * c + i], key[:, i * HD : (i + 1) * HD]) for i in range(2)]
    maps = [silu(m).astype(BF16) for m in maps]
    for i in range(2):
        kmapt[half, 2 * c + i] = maps[i]
        emit(2 * c + i, dot(maps[i], value[:, i * HD : (i + 1) * HD]))


def intra(half, c, attn, wq_v, fm_v, proj, qmap, kmapt, val, num):
    side = ROWS // 2
    causal = lax.broadcasted_iota(jnp.int32, (side, side), 0) >= lax.broadcasted_iota(
        jnp.int32, (side, side), 1
    )
    wide = slice(c * CHUNK, (c + 1) * CHUNK)
    proj[...] = dot(attn[...], wq_v[half, :, wide]).astype(BF16)
    for i in range(2):
        e = 2 * c + i
        cols = slice(e * HD, (e + 1) * HD)
        qmap[half, e] = silu(dot(proj[:, i * HD : (i + 1) * HD], fm_v[half, e])).astype(BF16)
        w00 = jnp.where(causal, dot(qmap[half, e, :side], kmapt[half, e, :, :side]), 0.0).astype(BF16)
        num[half, e, :side] = dot(w00, val[half, :side, cols])
        w10 = dot(qmap[half, e, side:], kmapt[half, e, :, :side]).astype(BF16)
        w11 = jnp.where(causal, dot(qmap[half, e, side:], kmapt[half, e, :, side:]), 0.0).astype(BF16)
        num[half, e, side:] = dot(w10, val[half, :side, cols]) + dot(w11, val[half, side:, cols])


def inter(half, e, qmap, prefix, num, attended):
    numerator = num[half, e] + dot(qmap[half, e], prefix[e])
    scale = lax.rsqrt(jnp.mean(numerator * numerator, axis=-1, keepdims=True) + 1e-06)
    attended[half, :, e * HD : (e + 1) * HD] = (numerator * scale).astype(BF16)


def out_part(half, heads, cols, attended, wo_v):
    part = slice(heads * CHUNK, (heads + 1) * CHUNK)
    return dot(attended[half, :, part], wo_v[half, part, cols])


def first_output(mid, attended, wo_v, acc):
    for c in range(4):
        cols = slice(c * CHUNK, (c + 1) * CHUNK)
        both = out_part(0, 0, cols, attended, wo_v) + out_part(1, 0, cols, attended, wo_v)
        acc[:, cols] = mid[:, cols].astype(F32) + both


def own_output(own, attended, wo_v, acc):
    for c in range(4):
        cols = slice(c * CHUNK, (c + 1) * CHUNK)
        acc[:, cols] += out_part(own, 1, cols, attended, wo_v)


def last_output(other, attended, wo_v, acc, out):
    for c in range(4):
        cols = slice(c * CHUNK, (c + 1) * CHUNK)
        out[:, cols] = (acc[:, cols] + out_part(other, 1, cols, attended, wo_v)).astype(BF16)


def kernel(
    sizes,
    frames, conv_in, taps, conv_out, wq, wk, wv, fm, wo, out,
    x_v, normed, w_in, tap_v, w_c, wq_v, wk_v, wv_v, fm_v, wo_v, fmt,
    glu, dw, act, mid, attn, proj, val, kmapt, num, qmap, acc, attended,
    st_own, p_send, p_recv, a_send, a_recv, y_send, y_recv, r_send, r_recv, pref, q_send, q_recv,
    load_sem, halo_s, halo_r, w_s, w_r, p_s, p_r, a_s, a_r, y_s, y_r, r_s, r_r, q_s, q_r,
):
    ny, nx, nz = sizes
    planes = nx * nz
    count = ny * planes * 2
    y, x, z, h = [lax.axis_index(a) for a in AXES]
    plane = x * nz + z
    lin = ((y * nx + x) * nz + z) * 2 + h
    other, own = 0, 1
    pair = (y, x, z, 1 - h)
    has_prev = lin > 0
    has_next = lin < count - 1

    def device(n):
        chip = lax.div(n, 2)
        column = lax.rem(chip, planes)
        return (lax.div(chip, planes), lax.div(column, nz), lax.rem(column, nz), lax.rem(n, 2))

    prev = device(lax.rem(lin + count - 1, count))
    following = device(lax.rem(lin + 1, count))

    def hops(offset):
        return sum(min(d, n - d) for d, n in zip(offset, (nx, nz)))

    offsets = [(i, j) for i in range(nx) for j in range(nz) if i or j]
    offsets.sort(key=hops, reverse=True)

    def plane_peer(offset):
        return (y, lax.rem(x + offset[0], nx), lax.rem(z + offset[1], nz), h)

    loads = []

    def load(src, dst):
        copy = pltpu.make_async_copy(src, dst, load_sem.at[len(loads)])
        copy.start()
        loads.append(copy)
        return copy

    ld_x = []
    for at in (pl.ds(0, ROWS // 2), pl.ds(ROWS // 2, ROWS // 2)):
        ld_x.append(load(frames.at[at], x_v.at[at]))
    ld_f = load(fm, fm_v.at[own])
    ld_in = []
    for c in range(8):
        at = (c % 2) * 4 + c // 2
        ld_in.append(load(conv_in.at[:, pl.ds(at * CHUNK, CHUNK)], w_in.at[at]))
    barrier = pltpu.get_barrier_semaphore()

    def greet(d):
        pl.semaphore_signal(barrier, inc=1, device_id=d, device_id_type=MESH)

    @pl.when(has_prev)
    def _():
        greet(prev)

    @pl.when(has_next)
    def _():
        greet(following)

    greet(pair)

    for k in offsets:
        greet(plane_peer(k))

    for k in range(1, ny):
        greet((lax.rem(y + k, ny), x, z, h))

    def remote(src, dst, s, r, d):
        return pltpu.make_async_remote_copy(
            src_ref=src, dst_ref=dst, send_sem=s, recv_sem=r, device_id=d, device_id_type=MESH
        )

    ld_x[0].wait()
    ld_tap = load(taps, tap_v)
    ld_c = load(conv_out, w_c)
    ld_k = load(wk, wk_v.at[own])
    ld_v = load(wv, wv_v.at[own])
    ld_q = load(wq, wq_v.at[own])
    ld_o = load(wo, wo_v.at[own])
    normalize(x_v, 0, 2, normed)
    ld_x[1].wait()
    normalize(x_v, 2, 4, normed)
    ld_f.wait()
    for e in range(HEADS):
        fmt[own, e] = fm_v[own, e].astype(F32).T.astype(BF16)
    for c in range(4):
        ld_in[2 * c].wait()
        ld_in[2 * c + 1].wait()
        gated(c, normed, w_in, glu)

    pl.semaphore_wait(
        barrier, 1 + planes - 1 + ny - 1 + has_prev.astype(jnp.int32) + has_next.astype(jnp.int32)
    )
    low = remote(
        glu.at[pl.ds(HALO, HALO)], glu.at[pl.ds(HALO + ROWS, HALO)], halo_s.at[0], halo_r.at[0], prev
    )
    high = remote(
        glu.at[pl.ds(ROWS, HALO)], glu.at[pl.ds(0, HALO)], halo_s.at[1], halo_r.at[1], following
    )

    @pl.when(has_prev)
    def _():
        low.start()

    @pl.when(has_next)
    def _():
        high.start()

    weights = []
    for i, (src, dst) in enumerate(((wk, wk_v), (wv, wv_v), (fmt.at[own], fmt), (fm, fm_v), (wq, wq_v), (wo, wo_v))):
        copy = remote(src, dst.at[other], w_s.at[i], w_r.at[i], pair)
        copy.start()
        weights.append(copy)

    ld_tap.wait()
    convolve_inner(glu, tap_v, dw)

    @pl.when(has_prev)
    def _():
        low.wait_send()
        high.wait_recv()

    @pl.when(has_next)
    def _():
        high.wait_send()
        low.wait_recv()

    @pl.when(jnp.logical_not(has_prev))
    def _():
        glu[pl.ds(0, HALO), :] = jnp.zeros((HALO, D), F32)

    @pl.when(jnp.logical_not(has_next))
    def _():
        glu[pl.ds(HALO + ROWS, HALO), :] = jnp.zeros((HALO, D), F32)

    convolve_edges(glu, tap_v, dw)
    activate(dw, act)

    ld_c.wait()
    conv_back(x_v, act, w_c, mid)
    normalize(mid, 0, ROWS // 128, attn)

    ld_k.wait()
    ld_v.wait()
    for copy in weights[:3]:
        copy.wait()

    def emit_other(e, s):
        p_send[e] = s.astype(BF16)

    def emit_own(e, s):
        st_own[e] = s

    def keys(half, c, emit):
        key_states(half, c, attn, wk_v, wv_v, fmt, val, kmapt, emit)

    def queries(half, c):
        intra(half, c, attn, wq_v, fm_v, proj, qmap, kmapt, val, num)

    piece = 2 * FEAT // planes
    per = planes // 2

    def p_copy(c):
        at = pl.ds(2 * c, 2)
        return remote(p_send.at[at], p_recv.at[at], p_s.at[c], p_r.at[c], pair)

    def q_copy(c):
        at = pl.ds(2 * c, 2)
        return remote(q_send.at[at], q_recv.at[at], q_s.at[c], q_r.at[c], pair)

    def a_copy(c, k):
        peer = plane_peer(k)
        p = peer[1] * nz + peer[2]
        return remote(a_send.at[c, p], a_recv.at[c, plane], a_s.at[c], a_r.at[c], peer)

    def r_copy(c, k):
        peer = plane_peer(k)
        p = peer[1] * nz + peer[2]
        return remote(r_send.at[c, p], r_recv.at[c, plane], r_s.at[c], r_r.at[c], peer)

    def y_copy(c, k):
        return remote(
            y_send.at[c], y_recv.at[c, k], y_s.at[c, k], y_r.at[c, k], (lax.rem(y + k, ny), x, z, h)
        )

    def a_start(c):
        p_copy(c).wait()
        for i in range(2):
            e = 2 * c + i
            chip_state = (st_own[e] + p_recv[e].astype(F32)).astype(BF16)
            a_send[c, i * per : (i + 1) * per] = chip_state.reshape(per, piece, HD)

        for k in offsets:
            a_copy(c, k).start()

        a_recv[c, plane] = a_send[c, plane]

    def y_start(c):
        every = pl.ds(0, planes - 1)
        pieces = remote(
            a_send.at[c, every], a_recv.at[c, every], a_s.at[c], a_r.at[c], plane_peer(offsets[0])
        )
        pieces.wait()

        run = a_recv[c, 0].astype(F32)
        for p in range(1, planes):
            run = run + a_recv[c, p].astype(F32)
        y_send[c] = run
        for k in range(1, ny):

            @pl.when(y + k < ny)
            def _():
                y_copy(c, k).start()

    def r_start(c):
        for k in range(1, ny):

            @pl.when(y + k < ny)
            def _():
                y_copy(c, k).wait_send()

            @pl.when(y >= k)
            def _():
                y_copy(c, k).wait_recv()

        run = jnp.zeros((piece, HD), F32)
        for k in range(1, ny):
            run = run + jnp.where(y >= k, y_recv[c, k], 0.0)
        for p in range(planes):
            r_send[c, p] = run.astype(BF16)
            run = run + a_recv[c, p].astype(F32)

        for k in offsets:
            r_copy(c, k).start()

        r_recv[c, plane] = r_send[c, plane]

    def q_start(c):
        every = pl.ds(0, planes - 1)
        pieces = remote(
            r_send.at[c, every], r_recv.at[c, every], r_s.at[c], r_r.at[c], plane_peer(offsets[0])
        )
        pieces.wait()

        for i in range(2):
            e = 2 * c + i
            before = r_recv[c, i * per : (i + 1) * per].reshape(FEAT, HD).astype(F32)
            q_send[e] = (before + jnp.where(h == 0, st_own[e], 0.0)).astype(BF16)
            pref[e] = (before + jnp.where(h == 1, p_recv[e].astype(F32), 0.0)).astype(BF16)
        q_copy(c).start()

    keys(other, 0, emit_other)
    p_copy(0).start()
    keys(own, 0, emit_own)
    a_start(0)
    keys(other, 1, emit_other)
    p_copy(1).start()
    keys(own, 1, emit_own)
    a_start(1)
    ld_q.wait()
    ld_o.wait()
    for copy in weights[3:]:
        copy.wait()
    queries(other, 0)
    y_start(0)
    queries(other, 1)
    y_start(1)
    r_start(0)
    queries(own, 0)
    r_start(1)
    queries(own, 1)
    q_start(0)
    inter(own, 0, qmap, pref, num, attended)
    inter(own, 1, qmap, pref, num, attended)
    q_copy(0).wait()
    inter(other, 0, qmap, q_recv, num, attended)
    inter(other, 1, qmap, q_recv, num, attended)
    first_output(mid, attended, wo_v, acc)
    q_start(1)
    inter(own, 2, qmap, pref, num, attended)
    inter(own, 3, qmap, pref, num, attended)
    own_output(own, attended, wo_v, acc)
    q_copy(1).wait()
    inter(other, 2, qmap, q_recv, num, attended)
    inter(other, 3, qmap, q_recv, num, attended)
    last_output(other, attended, wo_v, acc, out)


def shards(sizes, *args):
    ny, nx, nz = sizes
    planes = nx * nz
    piece = 2 * FEAT // planes
    dma = pltpu.SemaphoreType.DMA
    state = (HEADS, FEAT, HD)
    scratch = [
        pltpu.VMEM((ROWS, D), BF16),
        pltpu.VMEM((ROWS, D), BF16),
        pltpu.VMEM((8, D, CHUNK), BF16),
        pltpu.VMEM((TAPS, D), F32),
        pltpu.VMEM((D, D), BF16),
        pltpu.VMEM((2, D, HALF), BF16),
        pltpu.VMEM((2, D, HALF), BF16),
        pltpu.VMEM((2, D, HALF), BF16),
        pltpu.VMEM((2, HEADS, HD, FEAT), BF16),
        pltpu.VMEM((2, HALF, D), BF16),
        pltpu.VMEM((2, HEADS, FEAT, HD), BF16),
        pltpu.VMEM((PAD, D), F32),
        pltpu.VMEM((ROWS, D), F32),
        pltpu.VMEM((ROWS, D), BF16),
        pltpu.VMEM((ROWS, D), BF16),
        pltpu.VMEM((ROWS, D), BF16),
        pltpu.VMEM((ROWS, CHUNK), BF16),
        pltpu.VMEM((2, ROWS, HALF), BF16),
        pltpu.VMEM((2, HEADS, FEAT, ROWS), BF16),
        pltpu.VMEM((2, HEADS, ROWS, HD), F32),
        pltpu.VMEM((2, HEADS, ROWS, FEAT), BF16),
        pltpu.VMEM((ROWS, D), F32),
        pltpu.VMEM((2, ROWS, HALF), BF16),
        pltpu.VMEM(state, F32),
        pltpu.VMEM(state, BF16),
        pltpu.VMEM(state, BF16),
        pltpu.VMEM((2, planes, piece, HD), BF16),
        pltpu.VMEM((2, planes, piece, HD), BF16),
        pltpu.VMEM((2, piece, HD), F32),
        pltpu.VMEM((2, ny, piece, HD), F32),
        pltpu.VMEM((2, planes, piece, HD), BF16),
        pltpu.VMEM((2, planes, piece, HD), BF16),
        pltpu.VMEM(state, BF16),
        pltpu.VMEM(state, BF16),
        pltpu.VMEM(state, BF16),
        dma((17,)),
        dma((2,)),
        dma((2,)),
        dma((6,)),
        dma((6,)),
        dma((2,)),
        dma((2,)),
        dma((2,)),
        dma((2,)),
        dma((2, ny)),
        dma((2, ny)),
        dma((2,)),
        dma((2,)),
        dma((2,)),
        dma((2,)),
    ]
    return pl.pallas_call(
        functools.partial(kernel, sizes),
        out_shape=pltpu.VMEM((ROWS, D), BF16),
        in_specs=[pl.BlockSpec(memory_space=pl.ANY)] * 9,
        out_specs=pl.BlockSpec(memory_space=pltpu.VMEM),
        scratch_shapes=scratch,
        compiler_params=pltpu.CompilerParams(
            collective_id=0, has_side_effects=True, vmem_limit_bytes=56 * 1024 * 1024
        ),
        cost_estimate=pl.CostEstimate(
            flops=10_200_000_000, bytes_accessed=13_000_000, transcendentals=5_000_000
        ),
        name="block",
    )(*args)


def solution(mesh):
    side = round(mesh.shape["tm"] ** (1 / 3))
    sizes = (side, side, side)
    torus = Mesh(mesh.devices.reshape(*sizes, mesh.shape["head"]), AXES)
    rows = P(AXES, None)
    half = P(None, "head")
    in_specs = (rows, P(), P(), P(), half, half, half, P("head", None, None), P("head", None))
    return jax.shard_map(
        functools.partial(shards, sizes), mesh=torus, in_specs=in_specs, out_specs=rows, check_vma=False
    )
```

```python
import functools

import jax
import jax.numpy as jnp
from jax import lax
from jax.experimental import pallas as pl
from jax.experimental.pallas import tpu as pltpu
from jax.sharding import Mesh
from jax.sharding import PartitionSpec as P

AXES = ("tm_0", "tm_1", "tm_2", "head")
MESH = pl.DeviceIdType.MESH
BF16 = jnp.bfloat16
F32 = jnp.float32

ROWS = 512
D = 1024
HALO = 16
PAD = ROWS + 2 * HALO
HALF = 512
HEADS = 4
HD = 128
FEAT = 256
TAPS = 31
CHUNK = 256


def dot(a, b):
    return jnp.dot(a, b, preferred_element_type=F32)


def dot_nt(a, b):
    return lax.dot_general(a, b, (((1,), (1,)), ((), ())), preferred_element_type=F32)


def sigmoid(v):
    return 0.5 * jnp.tanh(0.5 * v) + 0.5


def silu(v):
    half = 0.5 * v
    return half * jnp.tanh(half) + half


def row_stats(read):
    total = read(0)
    for c in range(1, D // 128):
        total = total + read(c)
    mean = jnp.sum(total, axis=-1, keepdims=True) * (1.0 / D)
    spread = None
    for c in range(D // 128):
        center = read(c) - mean
        spread = center * center if spread is None else spread + center * center
    return mean, lax.rsqrt(jnp.sum(spread, axis=-1, keepdims=True) * (1.0 / D) + 1e-05)


def normalize(src, first, last, dst):
    for i in range(first, last):
        at = pl.ds(i * 128, 128)

        def read(c):
            return src[at, c * 128 : (c + 1) * 128].astype(F32)

        mean, scale = row_stats(read)
        for c in range(D // 128):
            dst[i * 128 : (i + 1) * 128, c * 128 : (c + 1) * 128] = ((read(c) - mean) * scale).astype(BF16)


def gated(c, normed, w_in, glu):
    value = dot(normed[...], w_in[c])
    gate = dot(normed[...], w_in[4 + c])
    glu[HALO : HALO + ROWS, c * CHUNK : (c + 1) * CHUNK] = (
        (value * sigmoid(gate)).astype(BF16).astype(F32)
    )


def convolve(base, count, glu, tap_v, dw):
    for c in range(D // 128):
        cols = slice(c * 128, (c + 1) * 128)
        window = glu[pl.ds(base, count + 32), cols]
        total = None
        for r in range(8):
            part = None
            for q in range(4):
                j = 8 * q + r - 1
                if j < 0:
                    continue
                term = window[8 * q : 8 * q + count + 8] * tap_v[j : j + 1, cols]
                part = term if part is None else part + term
            part = part[r : r + count]
            total = part if total is None else total + part
        dw[pl.ds(base, count), cols] = total


def convolve_inner(glu, tap_v, dw):
    @pl.loop(0, 3)
    def _(i):
        convolve(pl.multiple_of(64 + i * 128, 64), 128, glu, tap_v, dw)


def convolve_edges(glu, tap_v, dw):
    @pl.loop(0, 2)
    def _(i):
        convolve(pl.multiple_of(i * (ROWS - 64), 64), 64, glu, tap_v, dw)


def activate(first, last, dw, act):
    for i in range(first, last, 64):
        at = slice(i, i + 64)

        def read(c):
            return dw[at, c * 128 : (c + 1) * 128]

        mean, scale = row_stats(read)
        for c in range(D // 128):
            act[at, c * 128 : (c + 1) * 128] = silu((read(c) - mean) * scale).astype(BF16)


def conv_back(x, act, w_c, mid):
    for c in range(4):
        cols = slice(c * CHUNK, (c + 1) * CHUNK)
        mid[:, cols] = (x[:, cols].astype(F32) + dot(act[...], w_c[:, cols])).astype(BF16)


def key_states(half, c, attn, wk_v, wv_v, fmt, val, kmapt, emit):
    wide = slice(c * CHUNK, (c + 1) * CHUNK)
    key = dot(attn[...], wk_v[half, :, wide]).astype(BF16)
    value = dot(attn[...], wv_v[half, :, wide]).astype(BF16)
    val[half, :, wide] = value
    maps = [dot_nt(fmt[half, 2 * c + i], key[:, i * HD : (i + 1) * HD]) for i in range(2)]
    maps = [silu(m).astype(BF16) for m in maps]
    for i in range(2):
        kmapt[half, 2 * c + i] = maps[i]
        emit(2 * c + i, dot(maps[i], value[:, i * HD : (i + 1) * HD]))


def intra(half, c, attn, wq_v, fm_v, proj, qmap, kmapt, val, num):
    side = ROWS // 2
    causal = lax.broadcasted_iota(jnp.int32, (side, side), 0) >= lax.broadcasted_iota(
        jnp.int32, (side, side), 1
    )
    wide = slice(c * CHUNK, (c + 1) * CHUNK)
    proj[...] = dot(attn[...], wq_v[half, :, wide]).astype(BF16)
    for i in range(2):
        e = 2 * c + i
        cols = slice(e * HD, (e + 1) * HD)
        qmap[half, e] = silu(dot(proj[:, i * HD : (i + 1) * HD], fm_v[half, e])).astype(BF16)
        w00 = jnp.where(causal, dot(qmap[half, e, :side], kmapt[half, e, :, :side]), 0.0).astype(BF16)
        num[half, e, :side] = dot(w00, val[half, :side, cols])
        w10 = dot(qmap[half, e, side:], kmapt[half, e, :, :side]).astype(BF16)
        w11 = jnp.where(causal, dot(qmap[half, e, side:], kmapt[half, e, :, side:]), 0.0).astype(BF16)
        num[half, e, side:] = dot(w10, val[half, :side, cols]) + dot(w11, val[half, side:, cols])


def inter(half, e, qmap, prefix, num, attended):
    numerator = num[half, e] + dot(qmap[half, e], prefix[e])
    scale = lax.rsqrt(jnp.mean(numerator * numerator, axis=-1, keepdims=True) + 1e-06)
    attended[half, :, e * HD : (e + 1) * HD] = (numerator * scale).astype(BF16)


def out_part(half, heads, cols, attended, wo_v):
    part = slice(heads * CHUNK, (heads + 1) * CHUNK)
    return dot(attended[half, :, part], wo_v[half, part, cols])


def first_output(mid, attended, wo_v, acc):
    for c in range(4):
        cols = slice(c * CHUNK, (c + 1) * CHUNK)
        both = out_part(0, 0, cols, attended, wo_v) + out_part(1, 0, cols, attended, wo_v)
        acc[:, cols] = mid[:, cols].astype(F32) + both


def own_output(own, attended, wo_v, acc):
    for c in range(4):
        cols = slice(c * CHUNK, (c + 1) * CHUNK)
        acc[:, cols] += out_part(own, 1, cols, attended, wo_v)


def last_output(other, attended, wo_v, acc, out):
    for c in range(4):
        cols = slice(c * CHUNK, (c + 1) * CHUNK)
        out[:, cols] = (acc[:, cols] + out_part(other, 1, cols, attended, wo_v)).astype(BF16)


def kernel(
    sizes,
    frames, conv_in, taps, conv_out, wq, wk, wv, fm, wo, out,
    x_v, normed, w_in, tap_v, w_c, wq_v, wk_v, wv_v, fm_v, wo_v, fmt,
    glu, dw, act, mid, attn, proj, val, kmapt, num, qmap, acc, attended,
    st_own, p_send, p_recv, a_send, a_recv, y_send, y_recv, r_send, r_recv, pref, q_send, q_recv,
    load_sem, halo_s, halo_r, w_s, w_r, p_s, p_r, a_s, a_r, y_s, y_r, r_s, r_r, q_s, q_r,
):
    ny, nx, nz = sizes
    planes = nx * nz
    count = ny * planes * 2
    y, x, z, h = [lax.axis_index(a) for a in AXES]
    plane = x * nz + z
    lin = ((y * nx + x) * nz + z) * 2 + h
    other, own = 0, 1
    pair = (y, x, z, 1 - h)
    has_prev = lin > 0
    has_next = lin < count - 1

    def device(n):
        chip = lax.div(n, 2)
        column = lax.rem(chip, planes)
        return (lax.div(chip, planes), lax.div(column, nz), lax.rem(column, nz), lax.rem(n, 2))

    prev = device(lax.rem(lin + count - 1, count))
    following = device(lax.rem(lin + 1, count))

    def hops(offset):
        return sum(min(d, n - d) for d, n in zip(offset, (nx, nz)))

    offsets = [(i, j) for i in range(nx) for j in range(nz) if i or j]
    offsets.sort(key=hops, reverse=True)

    def plane_peer(offset):
        return (y, lax.rem(x + offset[0], nx), lax.rem(z + offset[1], nz), h)

    loads = []

    def load(src, dst):
        copy = pltpu.make_async_copy(src, dst, load_sem.at[len(loads)])
        copy.start()
        loads.append(copy)
        return copy

    ld_x = []
    for at in (pl.ds(0, ROWS // 2), pl.ds(ROWS // 2, ROWS // 2)):
        ld_x.append(load(frames.at[at], x_v.at[at]))
    ld_f = load(fm, fm_v.at[own])
    ld_in = []
    for c in range(8):
        at = (c % 2) * 4 + c // 2
        ld_in.append(load(conv_in.at[:, pl.ds(at * CHUNK, CHUNK)], w_in.at[at]))
    barrier = pltpu.get_barrier_semaphore()

    def greet(d):
        pl.semaphore_signal(barrier, inc=1, device_id=d, device_id_type=MESH)

    @pl.when(has_prev)
    def _():
        greet(prev)

    @pl.when(has_next)
    def _():
        greet(following)

    greet(pair)

    for k in offsets:
        greet(plane_peer(k))

    for k in range(1, ny):
        greet((lax.rem(y + k, ny), x, z, h))

    def remote(src, dst, s, r, d):
        return pltpu.make_async_remote_copy(
            src_ref=src, dst_ref=dst, send_sem=s, recv_sem=r, device_id=d, device_id_type=MESH
        )

    ld_x[0].wait()
    ld_tap = load(taps, tap_v)
    ld_c = load(conv_out, w_c)
    ld_k = load(wk, wk_v.at[own])
    ld_v = load(wv, wv_v.at[own])
    ld_q = load(wq, wq_v.at[own])
    ld_o = load(wo, wo_v.at[own])
    normalize(x_v, 0, 2, normed)
    ld_x[1].wait()
    normalize(x_v, 2, 4, normed)
    ld_f.wait()
    for e in range(HEADS):
        fmt[own, e] = fm_v[own, e].astype(F32).T.astype(BF16)
    for c in range(4):
        ld_in[2 * c].wait()
        ld_in[2 * c + 1].wait()
        gated(c, normed, w_in, glu)

    pl.semaphore_wait(
        barrier, 1 + planes - 1 + ny - 1 + has_prev.astype(jnp.int32) + has_next.astype(jnp.int32)
    )
    low = remote(
        glu.at[pl.ds(HALO, HALO)], glu.at[pl.ds(HALO + ROWS, HALO)], halo_s.at[0], halo_r.at[0], prev
    )
    high = remote(
        glu.at[pl.ds(ROWS, HALO)], glu.at[pl.ds(0, HALO)], halo_s.at[1], halo_r.at[1], following
    )

    @pl.when(has_prev)
    def _():
        low.start()

    @pl.when(has_next)
    def _():
        high.start()

    weights = []
    for i, (src, dst) in enumerate(((wk, wk_v), (wv, wv_v), (fmt.at[own], fmt), (fm, fm_v), (wq, wq_v), (wo, wo_v))):
        copy = remote(src, dst.at[other], w_s.at[i], w_r.at[i], pair)
        copy.start()
        weights.append(copy)

    ld_tap.wait()
    convolve_inner(glu, tap_v, dw)
    activate(64, ROWS - 64, dw, act)

    @pl.when(has_prev)
    def _():
        low.wait_send()
        high.wait_recv()

    @pl.when(has_next)
    def _():
        high.wait_send()
        low.wait_recv()

    @pl.when(jnp.logical_not(has_prev))
    def _():
        glu[pl.ds(0, HALO), :] = jnp.zeros((HALO, D), F32)

    @pl.when(jnp.logical_not(has_next))
    def _():
        glu[pl.ds(HALO + ROWS, HALO), :] = jnp.zeros((HALO, D), F32)

    convolve_edges(glu, tap_v, dw)
    activate(0, 64, dw, act)
    activate(ROWS - 64, ROWS, dw, act)

    ld_c.wait()
    conv_back(x_v, act, w_c, mid)
    normalize(mid, 0, ROWS // 128, attn)

    ld_k.wait()
    ld_v.wait()
    for copy in weights[:3]:
        copy.wait()

    def emit_other(e, s):
        p_send[e] = s.astype(BF16)

    def emit_own(e, s):
        st_own[e] = s

    def keys(half, c, emit):
        key_states(half, c, attn, wk_v, wv_v, fmt, val, kmapt, emit)

    def queries(half, c):
        intra(half, c, attn, wq_v, fm_v, proj, qmap, kmapt, val, num)

    piece = 2 * FEAT // planes
    per = planes // 2

    def p_copy(c):
        at = pl.ds(2 * c, 2)
        return remote(p_send.at[at], p_recv.at[at], p_s.at[c], p_r.at[c], pair)

    def q_copy(c):
        at = pl.ds(2 * c, 2)
        return remote(q_send.at[at], q_recv.at[at], q_s.at[c], q_r.at[c], pair)

    def a_copy(c, k):
        peer = plane_peer(k)
        p = peer[1] * nz + peer[2]
        return remote(a_send.at[c, p], a_recv.at[c, plane], a_s.at[c], a_r.at[c], peer)

    def r_copy(c, k):
        peer = plane_peer(k)
        p = peer[1] * nz + peer[2]
        return remote(r_send.at[c, p], r_recv.at[c, plane], r_s.at[c], r_r.at[c], peer)

    def y_copy(c, k):
        return remote(
            y_send.at[c], y_recv.at[c, k], y_s.at[c, k], y_r.at[c, k], (lax.rem(y + k, ny), x, z, h)
        )

    def a_start(c):
        p_copy(c).wait()
        for i in range(2):
            e = 2 * c + i
            chip_state = (st_own[e] + p_recv[e].astype(F32)).astype(BF16)
            a_send[c, i * per : (i + 1) * per] = chip_state.reshape(per, piece, HD)

        for k in offsets:
            a_copy(c, k).start()

        a_recv[c, plane] = a_send[c, plane]

    def y_start(c):
        every = pl.ds(0, planes - 1)
        pieces = remote(
            a_send.at[c, every], a_recv.at[c, every], a_s.at[c], a_r.at[c], plane_peer(offsets[0])
        )
        pieces.wait()

        run = a_recv[c, 0].astype(F32)
        for p in range(1, planes):
            run = run + a_recv[c, p].astype(F32)
        y_send[c] = run
        for k in range(1, ny):

            @pl.when(y + k < ny)
            def _():
                y_copy(c, k).start()

    def r_start(c):
        for k in range(1, ny):

            @pl.when(y + k < ny)
            def _():
                y_copy(c, k).wait_send()

            @pl.when(y >= k)
            def _():
                y_copy(c, k).wait_recv()

        run = jnp.zeros((piece, HD), F32)
        for k in range(1, ny):
            run = run + jnp.where(y >= k, y_recv[c, k], 0.0)
        for p in range(planes):
            r_send[c, p] = run.astype(BF16)
            run = run + a_recv[c, p].astype(F32)

        for k in offsets:
            r_copy(c, k).start()

        r_recv[c, plane] = r_send[c, plane]

    def q_start(c):
        every = pl.ds(0, planes - 1)
        pieces = remote(
            r_send.at[c, every], r_recv.at[c, every], r_s.at[c], r_r.at[c], plane_peer(offsets[0])
        )
        pieces.wait()

        for i in range(2):
            e = 2 * c + i
            before = r_recv[c, i * per : (i + 1) * per].reshape(FEAT, HD).astype(F32)
            q_send[e] = (before + jnp.where(h == 0, st_own[e], 0.0)).astype(BF16)
            pref[e] = (before + jnp.where(h == 1, p_recv[e].astype(F32), 0.0)).astype(BF16)
        q_copy(c).start()

    keys(other, 0, emit_other)
    p_copy(0).start()
    keys(own, 0, emit_own)
    a_start(0)
    keys(other, 1, emit_other)
    p_copy(1).start()
    keys(own, 1, emit_own)
    a_start(1)
    ld_q.wait()
    ld_o.wait()
    for copy in weights[3:]:
        copy.wait()
    queries(other, 0)
    y_start(0)
    queries(other, 1)
    y_start(1)
    r_start(0)
    queries(own, 0)
    r_start(1)
    queries(own, 1)
    q_start(0)
    inter(own, 0, qmap, pref, num, attended)
    inter(own, 1, qmap, pref, num, attended)
    q_copy(0).wait()
    inter(other, 0, qmap, q_recv, num, attended)
    inter(other, 1, qmap, q_recv, num, attended)
    first_output(mid, attended, wo_v, acc)
    q_start(1)
    inter(own, 2, qmap, pref, num, attended)
    inter(own, 3, qmap, pref, num, attended)
    own_output(own, attended, wo_v, acc)
    q_copy(1).wait()
    inter(other, 2, qmap, q_recv, num, attended)
    inter(other, 3, qmap, q_recv, num, attended)
    last_output(other, attended, wo_v, acc, out)


def shards(sizes, *args):
    ny, nx, nz = sizes
    planes = nx * nz
    piece = 2 * FEAT // planes
    dma = pltpu.SemaphoreType.DMA
    state = (HEADS, FEAT, HD)
    scratch = [
        pltpu.VMEM((ROWS, D), BF16),
        pltpu.VMEM((ROWS, D), BF16),
        pltpu.VMEM((8, D, CHUNK), BF16),
        pltpu.VMEM((TAPS, D), F32),
        pltpu.VMEM((D, D), BF16),
        pltpu.VMEM((2, D, HALF), BF16),
        pltpu.VMEM((2, D, HALF), BF16),
        pltpu.VMEM((2, D, HALF), BF16),
        pltpu.VMEM((2, HEADS, HD, FEAT), BF16),
        pltpu.VMEM((2, HALF, D), BF16),
        pltpu.VMEM((2, HEADS, FEAT, HD), BF16),
        pltpu.VMEM((PAD, D), F32),
        pltpu.VMEM((ROWS, D), F32),
        pltpu.VMEM((ROWS, D), BF16),
        pltpu.VMEM((ROWS, D), BF16),
        pltpu.VMEM((ROWS, D), BF16),
        pltpu.VMEM((ROWS, CHUNK), BF16),
        pltpu.VMEM((2, ROWS, HALF), BF16),
        pltpu.VMEM((2, HEADS, FEAT, ROWS), BF16),
        pltpu.VMEM((2, HEADS, ROWS, HD), F32),
        pltpu.VMEM((2, HEADS, ROWS, FEAT), BF16),
        pltpu.VMEM((ROWS, D), F32),
        pltpu.VMEM((2, ROWS, HALF), BF16),
        pltpu.VMEM(state, F32),
        pltpu.VMEM(state, BF16),
        pltpu.VMEM(state, BF16),
        pltpu.VMEM((2, planes, piece, HD), BF16),
        pltpu.VMEM((2, planes, piece, HD), BF16),
        pltpu.VMEM((2, piece, HD), F32),
        pltpu.VMEM((2, ny, piece, HD), F32),
        pltpu.VMEM((2, planes, piece, HD), BF16),
        pltpu.VMEM((2, planes, piece, HD), BF16),
        pltpu.VMEM(state, BF16),
        pltpu.VMEM(state, BF16),
        pltpu.VMEM(state, BF16),
        dma((17,)),
        dma((2,)),
        dma((2,)),
        dma((6,)),
        dma((6,)),
        dma((2,)),
        dma((2,)),
        dma((2,)),
        dma((2,)),
        dma((2, ny)),
        dma((2, ny)),
        dma((2,)),
        dma((2,)),
        dma((2,)),
        dma((2,)),
    ]
    return pl.pallas_call(
        functools.partial(kernel, sizes),
        out_shape=pltpu.VMEM((ROWS, D), BF16),
        in_specs=[pl.BlockSpec(memory_space=pl.ANY)] * 9,
        out_specs=pl.BlockSpec(memory_space=pltpu.VMEM),
        scratch_shapes=scratch,
        compiler_params=pltpu.CompilerParams(
            collective_id=0, has_side_effects=True, vmem_limit_bytes=56 * 1024 * 1024
        ),
        cost_estimate=pl.CostEstimate(
            flops=10_200_000_000, bytes_accessed=13_000_000, transcendentals=5_000_000
        ),
        name="block",
    )(*args)


def solution(mesh):
    side = round(mesh.shape["tm"] ** (1 / 3))
    sizes = (side, side, side)
    torus = Mesh(mesh.devices.reshape(*sizes, mesh.shape["head"]), AXES)
    rows = P(AXES, None)
    half = P(None, "head")
    in_specs = (rows, P(), P(), P(), half, half, half, P("head", None, None), P("head", None))
    return jax.shard_map(
        functools.partial(shards, sizes), mesh=torus, in_specs=in_specs, out_specs=rows, check_vma=False
    )
```
